512 devices in a mesh: dp: 128 (over x, z, core), rep: 4 (over y).
Axes of the slice: x: 4, y: 4, z: 16, core: 2. Of those that a mesh axis runs over, the one named last changes fastest.
Arguments:
- ratings: bfloat16 [1024, 12800], P(('dp', 'rep')), may hold values from -6 to 6
- confidence: bfloat16 [1024, 12800], P(('dp', 'rep')), may hold values from 1 to 20
- rated: int32 [1024, 200], P(('dp', 'rep')), may hold values 0 or 1
- item_factors: bfloat16 [1048576, 128], P(('dp', 'rep')), may hold values from -0.0546875 to 0.0546875
- cold_owner: int32 [128, 4, 192, 1], P('dp', 'rep'), may hold values from 0 to 127; in each aligned block of 192 rows (0 to 191, 192 to 383, ..., all dimensions but the last counted through in order) at most 2 rows name the same one
- cold_local: int32 [128, 4, 192], P('dp', 'rep'), may hold values from 0 to 127
- hot_group: int32 [8], replicated, may hold values from 0 to 127, as said below
- hot_local: int32 [8], replicated, may hold values from 0 to 127
Outputs:
- user_factors: float32 [1024, 128], P(('dp', 'rep'))
The draws below stay inside these ranges and needn't reach their ends.
Inputs may be any that keep to these rules, and one draw needn't show every extreme that they name: `cold_owner`: on each device, no owner group is named by more than 2 of its 192 rows; some group is named exactly 2 times. `hot_group`: the hot blocks' owner groups are distinct.
All inputs are finite; a program needn't handle non-finite values. No bound on the sum of `rated` on one device may be relied on, other than what follows from the above.
Results may differ from the reference program's by a relative error of at most 0.0029.
Values may be sent and summed in bfloat16 or wider, within the bound.
A program may use at most 64 MiB of HBM per device.

```python
import math
import jax
import jax.numpy as jnp
import numpy as np
from jax import lax

R = 128
BLK = 64
CAP = 2
HOT = 8
U_DEV = 2
ITERS = 3
NB_COLD = 192
NB = 200
GROUP_BLK = 128
ITEMS = 1048576
USERS = 1024
N_DP = 128
N_REP = 4


def draw_hot_group(key, part):
    return jax.random.permutation(key, N_DP)[:HOT].astype(jnp.int32)


def place_ends(result, stream_key, least, high):
    extent = result.shape
    place = [jax.random.randint(jax.random.fold_in(stream_key, axis), (), 0, extent[axis]) for axis in range(len(extent))]
    result = result.at[tuple(place)].set(least)
    longest = extent.index(max(extent))
    place[longest] = (place[longest] + 1) % extent[longest]
    return result.at[tuple(place)].set(high)


def block_scale(rng, dims, cuts, least, largest):
    def one(position, shards_of):
        steps = jax.random.uniform(jax.random.fold_in(jax.random.fold_in(rng, 6), position), (shards_of,), jnp.float32, least / len(cuts), largest / len(cuts))
        return jnp.repeat(jnp.exp(steps), dims[position] // shards_of).reshape((-1,) + (1,) * (len(dims) - position - 1))

    level = one(*cuts[0])
    for cut in cuts[1:]:
        level = level * one(*cut)
    return level


def assign_block(key, own, number, rows, count, top, most, lean):
    order = jax.random.permutation(key, count)
    heavy_load, ordinary = load_shares(count, rows * top, most, lean, True), load_shares(count, rows * top, most, lean, False)
    places = jnp.arange(count)

    def named(lengths, offset_by):
        used = int((lengths > 0).sum())
        fixed = max(1, used // 4)
        moved = fixed + (places - fixed + offset_by * (used - fixed)) % max(1, count - fixed)
        return jnp.zeros((count,), jnp.int32).at[order[jnp.where(places < fixed, places, moved)]].set(jnp.asarray(lengths, jnp.int32))

    lengths = jnp.where(number % 4 == 0, named(heavy_load, number // 4), named(ordinary, number - number // 4 - 1))
    mixed = jax.random.permutation(jax.random.fold_in(own, 3), count)
    giver, sink = mixed[0:count // 2 * 2:2], mixed[1:count // 2 * 2:2]
    room = jnp.minimum(lengths[giver] - 1, most - lengths[sink]) // 2
    room = jnp.where((giver == order[0]) | (sink == order[0]) | (lengths[sink] == 0), 0, jnp.maximum(room, 0))
    moved = jax.random.randint(jax.random.fold_in(own, 4), (count // 2,), 0, 1 << 20) % (room + 1)
    lengths = lengths.at[giver].add(-moved).at[sink].add(moved)
    members = jnp.searchsorted(jnp.cumsum(lengths), jnp.arange(rows * top), side="right").astype(jnp.int32)
    listing = members.reshape(top, rows).T
    listing = listing[jax.random.permutation(jax.random.fold_in(own, 1), rows)]
    offset_by = jax.random.randint(jax.random.fold_in(own, 2), (rows, 1), 0, top)
    return jnp.take_along_axis(listing, (jnp.arange(top)[None, :] + offset_by) % top, axis=1)


def load_shares(number_of, total, reach, lean, full):
    loads = [(1 << 20) // math.isqrt(standing ** lean) + 1 for standing in range(1, number_of + 1)]
    largest = reach if full else min(reach, max(-(-total // number_of), total * loads[0] // sum(loads)))
    least = 1 if total - largest >= number_of - 1 else 0
    counts, spare = [largest] + [least] * (number_of - 1), total - largest - least * (number_of - 1)
    while spare > 0:
        candidates = [i for i in range(1, number_of) if counts[i] < largest] or [i for i in range(1, number_of) if counts[i] < reach]
        mass, budget = sum([loads[i] for i in candidates]), spare
        for i in candidates:
            more = min(reach - counts[i], max(1, budget * loads[i] // mass), spare)
            counts[i] = counts[i] + more
            spare = spare - more
    return np.array(counts)


def scatter_about(rng, extent, deviation, limit, split=(), held_as=jnp.bfloat16):
    entries = deviation * jax.random.normal(rng, extent, jnp.float32)
    if split:
        entries = entries * block_scale(rng, extent, split, -0.22, 0.18)
    return jnp.clip(entries, -limit, limit).astype(held_as)


def setup_inputs(seed: int = 0) -> dict:
    keys = jax.random.split(jax.random.key(seed), 9)
    ratings = scatter_about(keys[0], (USERS, NB * BLK), 1.0, 6.0, ((0, 512),))
    confidence = jnp.clip(jnp.exp(math.log(20.0) - 2.9957323 * jax.random.uniform(keys[1], (USERS, NB * BLK), jnp.float32) ** block_scale(keys[1], (USERS, NB * BLK), ((0, 512),), -0.2, 0.2)), 1.0, 20.0).astype(jnp.bfloat16)
    rated = place_ends((jax.random.randint(keys[2], (USERS, NB), 0, 4) < 3).astype(jnp.int32), jax.random.fold_in(keys[2], 1), 0, 1)
    item_factors = scatter_about(keys[3], (ITEMS, R), (NB * BLK) ** -0.5, 0.0546875, ((0, 512),))
    cold_owner_keys = jax.random.split(jax.random.fold_in(keys[4], 1), N_DP * N_REP * NB_COLD // NB_COLD)
    cold_owner_turns = jax.random.permutation(jax.random.fold_in(keys[4], 3), N_DP * N_REP * NB_COLD // NB_COLD)
    cold_owner = jax.vmap(lambda own, number: assign_block(jax.random.fold_in(keys[4], 2), own, number, NB_COLD, N_DP, 1, CAP, 2))(cold_owner_keys, cold_owner_turns).reshape((N_DP, N_REP, NB_COLD, 1))
    cold_local = place_ends(jax.random.randint(keys[5], (N_DP, N_REP, NB_COLD), 0, GROUP_BLK), jax.random.fold_in(keys[5], 1), 0, GROUP_BLK - 1).astype(jnp.int32)
    hot_group = draw_hot_group(jax.random.fold_in(keys[8], 71), 0)
    hot_local = place_ends(jax.random.randint(keys[7], (HOT,), 0, GROUP_BLK), jax.random.fold_in(keys[7], 1), 0, GROUP_BLK - 1).astype(jnp.int32)
    return dict(ratings=ratings, confidence=confidence, rated=rated, item_factors=item_factors, cold_owner=cold_owner, cold_local=cold_local, hot_group=hot_group, hot_local=hot_local)


def conjugate(gram_stack, right_side):
    highest = lax.Precision.HIGHEST
    solution = jnp.zeros_like(right_side)
    residual = right_side
    direction = right_side
    norm_now = jnp.sum(residual * residual, axis=-1)
    for iteration in range(ITERS):
        images = jnp.einsum("urs,us->ur", gram_stack, direction, precision=highest)
        step_size = norm_now / jnp.sum(direction * images, axis=-1)
        solution = solution + step_size[:, None] * direction
        residual = residual - step_size[:, None] * images
        norm_next = jnp.sum(residual * residual, axis=-1)
        direction = residual + (norm_next / norm_now)[:, None] * direction
        norm_now = norm_next
    return solution


def tile_solve(item_rows, ratings, confidence, rated):
    user_count = confidence.shape[0]
    weights = (confidence.astype(jnp.float32).reshape(user_count, -1, BLK) * rated.astype(jnp.float32)[:, :, None]).reshape(user_count, -1)

    def one_user(user_pair):
        weight_row, rating_row = user_pair
        scaled = (weight_row[:, None] * item_rows.astype(jnp.float32)).astype(jnp.bfloat16)
        gram_matrix = jnp.dot(scaled.T, item_rows, preferred_element_type=jnp.float32)
        right_side = jnp.dot(rating_row, scaled, preferred_element_type=jnp.float32)
        return gram_matrix, right_side

    gram_stack, right_side = lax.map(one_user, (weights, ratings))
    gram_stack = gram_stack + 0.1 * jnp.eye(R, dtype=jnp.float32)[None, :, :]
    return conjugate(gram_stack, right_side)


def reference(ratings, confidence, rated, item_factors, cold_owner, cold_local, hot_group, hot_local):
    tile_count = N_DP * N_REP
    blocks = item_factors.reshape(-1, BLK * R)
    cold_ids = (cold_owner.reshape(tile_count, -1) * GROUP_BLK + cold_local.reshape(tile_count, -1)).astype(jnp.int32)
    hot_ids = (hot_group * GROUP_BLK + hot_local).astype(jnp.int32)
    hot_items = jnp.take(blocks, hot_ids, axis=0)

    def per_tile(tile_args):
        tile_ids, tile_ratings, tile_confidence, tile_rated = tile_args
        item_rows = jnp.concatenate([jnp.take(blocks, tile_ids, axis=0), hot_items], axis=0).reshape(-1, R)
        return tile_solve(item_rows, tile_ratings, tile_confidence, tile_rated)

    solved = lax.map(per_tile, (cold_ids, ratings.reshape(tile_count, U_DEV, -1), confidence.reshape(tile_count, U_DEV, -1), rated.reshape(tile_count, U_DEV, -1)))
    return solved.reshape(-1, R)
```

```python
import functools

import jax
import jax.numpy as jnp
from jax import lax
from jax.experimental import pallas as pl
from jax.experimental.pallas import tpu as pltpu
from jax.sharding import PartitionSpec as P

BLK = 64
CAP = 2
ITERS = 3
N_X = 4
MESH = pl.DeviceIdType.MESH
bf16, f32, i32 = jnp.bfloat16, jnp.float32, jnp.int32


def prepare(n_x, n_z, ratings, confidence, rated, cold_owner, cold_local, hot_group):
    pairs = n_x * n_z
    owners = cold_owner.reshape(-1)
    local_ids = cold_local.reshape(-1)
    cold = owners.shape[0]
    order = jnp.arange(cold, dtype=i32)
    same = (owners[:, None] == owners[None, :]) & (order[None, :] < order[:, None])
    slot_of = jnp.sum(same.astype(i32), axis=1)
    position = owners * CAP + slot_of
    match = position[None, :] == jnp.arange(2 * pairs * CAP, dtype=i32)[:, None]
    users = confidence.shape[0]
    weights = confidence.reshape(users, -1, BLK) * rated.astype(bf16)[:, :, None]
    both = jnp.concatenate([weights, ratings.reshape(users, -1, BLK)], axis=0)
    both = both.transpose(1, 0, 2).reshape(-1, 2 * users * BLK)
    cold_part = jnp.dot(match.astype(bf16), both[:cold], preferred_element_type=f32).astype(bf16)
    cold_part = cold_part.reshape(n_x, n_z, 2 * CAP, 2 * users, BLK).transpose(1, 0, 3, 2, 4)
    cold_part = cold_part.reshape(n_z, n_x, 2 * users, CAP, 2 * BLK)
    hot_match = hot_group[None, :] == jnp.arange(2 * pairs, dtype=i32)[:, None]
    hot_part = jnp.dot(hot_match.astype(bf16), both[cold:], preferred_element_type=f32).astype(bf16)
    hot_part = hot_part.reshape(n_x, n_z, 2, 2 * users, BLK).transpose(1, 0, 3, 2, 4)
    hot_part = hot_part.reshape(n_z, n_x, 2 * users, 1, 2 * BLK)
    message = jnp.concatenate([cold_part, hot_part], axis=3).reshape(n_z, n_x, 6 * users, 2 * BLK)
    message = jnp.pad(message, ((0, 0), (0, 0), (0, 16 - 6 * users), (0, 0)))
    ids = jnp.sum(jnp.where(match, local_ids[None, :], 0), axis=1)
    ids = ids.reshape(n_x, n_z, 1, 2 * CAP).transpose(1, 0, 2, 3)
    ids = jnp.pad(ids, ((0, 0), (0, 0), (0, 0), (0, 128 - 2 * CAP)))
    return message, ids


def kernel(n_x, n_z, message, ids, items, hot_id, out,
           table, msg_z, msg_x, ids_z, ids_x, ids_s, gram, part, mid, red_x, red_z, dir_z, dir_x,
           y_send, y_recv, c_send, c_recv, l_sem,
           a_send, a_recv, b_send, b_recv, zs_sem, zr_sem, xs_sem, xr_sem):
    dp = lax.axis_index("dp")
    y = lax.axis_index("rep")
    core = dp % 2
    z = (dp // 2) % n_z
    x = dp // (2 * n_z)
    n_y = 4

    def at(x_to, z_to):
        return ((x_to * n_z + z_to) * 2 + core, y)

    up, down, far = (y + 1) % n_y, (y + n_y - 1) % n_y, (y + 2) % n_y
    up_id, down_id, mate_id = (dp, up), (dp, down), (x * n_z * 2 + z * 2 + 1 - core, y)

    def remote(src, dst, send, recv, to):
        return pltpu.make_async_remote_copy(
            src_ref=src, dst_ref=dst, send_sem=send, recv_sem=recv, device_id=to, device_id_type=MESH)

    def each(count, body):
        for k in range(1, count):
            body(k)

    def others(ref, lead=()):
        index = lead + (pl.ds(0, ref.shape[len(lead)] - 1),)
        return ref.at[index]

    def waiter(ref, send, recv):
        return remote(ref, ref, send, recv, mate_id)

    barrier = pltpu.get_barrier_semaphore()
    for to in (up_id, down_id, mate_id):
        pl.semaphore_signal(barrier, inc=1, device_id=to, device_id_type=MESH)
    each(n_z, lambda k: pl.semaphore_signal(
        barrier, inc=1, device_id=at(x, (z + k) % n_z), device_id_type=MESH))
    each(n_x, lambda k: pl.semaphore_signal(
        barrier, inc=1, device_id=at((x + k) % n_x, z), device_id_type=MESH))
    pl.semaphore_wait(barrier, 3 + n_z - 1 + n_x - 1)

    held = items.shape[0]
    half = held // 2

    def rows(of_core, of_y, h):
        return table.at[of_core, pl.ds(of_y * held + h * half, half)]

    def own(h):
        return items.at[pl.ds(h * half, half)]

    def up_copy(k):
        if k < 2:
            return remote(own(k), rows(core, y, k), y_send.at[k], y_recv.at[k], up_id)
        return remote(rows(core, down, 0), rows(core, down, 0), y_send.at[2], y_recv.at[2], up_id)

    def down_copy(k):
        if k < 2:
            return remote(own(1 - k), rows(core, y, 1 - k), y_send.at[3 + k], y_recv.at[3 + k], down_id)
        return remote(rows(core, up, 1), rows(core, up, 1), y_send.at[5], y_recv.at[5], down_id)

    def from_down(k):
        ref = rows(core, down, k) if k < 2 else rows(core, far, 0)
        return remote(ref, ref, y_send.at[k], y_recv.at[k], up_id)

    def from_up(k):
        ref = rows(core, up, 1 - k) if k < 2 else rows(core, far, 1)
        return remote(ref, ref, y_send.at[3 + k], y_recv.at[3 + k], down_id)

    def mate_copy(n, src, of_y, h):
        return remote(src, rows(core, of_y, h), c_send.at[n], c_recv.at[n], mate_id)

    def from_mate(n, of_y, h):
        ref = rows(1 - core, of_y, h)
        return remote(ref, ref, c_send.at[n], c_recv.at[n], mate_id)

    for k in range(2):
        up_copy(k).start()
        down_copy(k).start()
    keep = pltpu.make_async_copy(items, table.at[core, pl.ds(y * held, held)], l_sem.at[0])
    keep.start()

    def start_z(k):
        to = (z + k) % n_z
        remote(message.at[to], msg_z.at[z], a_send.at[0], a_recv.at[0], at(x, to)).start()
        remote(ids.at[to], ids_z.at[z], a_send.at[1], a_recv.at[1], at(x, to)).start()

    def start_x(k):
        to = (x + k) % n_x
        remote(msg_z.at[:, to], msg_x.at[x], b_send.at[0], b_recv.at[0], at(to, z)).start()
        remote(ids_z.at[:, to], ids_x.at[x], b_send.at[1], b_recv.at[1], at(to, z)).start()

    z_done = [waiter(others(msg_z), a_send.at[0], a_recv.at[0]), waiter(others(ids_z), a_send.at[1], a_recv.at[1])]
    x_done = [waiter(others(msg_x), b_send.at[0], b_recv.at[0]), waiter(others(ids_x), b_send.at[1], b_recv.at[1])]

    each(n_z, start_z)
    for h in range(2):
        mate_copy(h, own(h), y, h).start()
    msg_z[z] = message[z]
    ids_z[z] = ids[z]

    from_down(0).wait_recv()
    up_copy(2).start()
    from_up(0).wait_recv()
    down_copy(2).start()
    mate_copy(2, rows(core, down, 0), down, 0).start()
    mate_copy(3, rows(core, up, 1), up, 1).start()

    for copy in z_done:
        copy.wait_recv()
    each(n_x, start_x)
    msg_x[x] = msg_z[:, x]
    ids_x[x] = ids_z[:, x]

    from_down(1).wait_recv()
    mate_copy(4, rows(core, down, 1), down, 1).start()
    from_up(1).wait_recv()
    mate_copy(5, rows(core, up, 0), up, 0).start()

    for copy in x_done:
        copy.wait_recv()
    to_smem = pltpu.make_async_copy(ids_x, ids_s, l_sem.at[1])
    to_smem.start()

    from_down(2).wait_recv()
    mate_copy(6, rows(core, far, 0), far, 0).start()
    from_up(2).wait_recv()
    mate_copy(7, rows(core, far, 1), far, 1).start()

    for copy in z_done + x_done:
        copy.wait_send()
    for k in range(3):
        up_copy(k).wait_send()
        down_copy(k).wait_send()
    halves = [(y, 0), (y, 1), (down, 0), (up, 1), (down, 1), (up, 0), (far, 0), (far, 1)]
    for n, (of_y, h) in enumerate(halves):
        mate_copy(n, rows(core, of_y, h), of_y, h).wait_send()
    for n, (of_y, h) in enumerate(halves):
        from_mate(n, of_y, h).wait_recv()
    keep.wait()
    to_smem.wait()

    hot_rows = [table[0, hot_id[0]], table[1, hot_id[1]]]
    row_of = lax.broadcasted_iota(i32, (16, 128), 0)
    masks = [((row_of == 6 + j) | (row_of == 9 + j)).astype(f32) for j in range(3)]

    def build(t, carry):
        xt, zt = t // n_z, t % n_z
        found = [table[s // CAP, ids_s[xt, zt, 0, s]] for s in range(2 * CAP)] + hot_rows
        chosen = jnp.concatenate(found, axis=0).T
        text = msg_x[xt, zt].astype(f32)
        scaled = []
        for u in range(2):
            weight = jnp.concatenate(
                [jnp.broadcast_to(text[3 * u + j:3 * u + j + 1], (128, 128)) for j in range(3)], axis=1)
            scaled.append(chosen * weight.astype(bf16))
        scaled = jnp.concatenate(scaled, axis=0)
        rating = jnp.concatenate([(text * masks[j]).astype(bf16) for j in range(3)], axis=1)
        left = jnp.concatenate([chosen, rating], axis=0)
        both = lax.dot_general(left, scaled, (((1,), (1,)), ((), ())), preferred_element_type=f32)
        for u in range(2):
            gram[2 * t + u] = both[:128, 128 * u:128 * u + 128]
            lot = both[128 + 6 + 3 * u:128 + 9 + 3 * u, 128 * u:128 * u + 128]
            part[ITERS, xt, zt, pl.ds(u, 1), :] = jnp.sum(lot, axis=0, keepdims=True)
        return carry

    lax.fori_loop(0, n_x * n_z, build, 0)

    def reduce(slot):
        def x_start(k):
            to = (x + k) % n_x
            remote(part.at[slot, to], red_x.at[slot, x], xs_sem.at[0, slot], xr_sem.at[0, slot], at(to, z)).start()

        def z_start(k):
            to = (z + k) % n_z
            remote(mid.at[slot, to], red_z.at[slot, z], zs_sem.at[0, slot], zr_sem.at[0, slot], at(x, to)).start()

        each(n_x, x_start)
        red_x[slot, x] = part[slot, x]
        reduced_x(slot).wait_recv()
        mid[slot] = jnp.sum(red_x[slot], axis=0)
        each(n_z, z_start)
        red_z[slot, z] = mid[slot, z]
        reduced_z(slot).wait_recv()
        return jnp.sum(red_z[slot], axis=0)

    def reduced_x(slot):
        return waiter(others(red_x, (slot,)), xs_sem.at[0, slot], xr_sem.at[0, slot])

    def reduced_z(slot):
        return waiter(others(red_z, (slot,)), zs_sem.at[0, slot], zr_sem.at[0, slot])

    def gather(slot, value):
        dir_z[slot, z] = value

        def z_start(k):
            own_dir = dir_z.at[slot, z]
            remote(own_dir, own_dir, zs_sem.at[1, slot], zr_sem.at[1, slot], at(x, (z + k) % n_z)).start()

        def x_start(k):
            remote(dir_z.at[slot], dir_x.at[slot, x], xs_sem.at[1, slot], xr_sem.at[1, slot], at((x + k) % n_x, z)).start()

        each(n_z, z_start)
        gathered_z(slot).wait_recv()
        each(n_x, x_start)
        dir_x[slot, x] = dir_z[slot]
        gathered_x(slot).wait_recv()

    def gathered_z(slot):
        return waiter(others(dir_z, (slot,)), zs_sem.at[1, slot], zr_sem.at[1, slot])

    def gathered_x(slot):
        return waiter(others(dir_x, (slot,)), xs_sem.at[1, slot], xr_sem.at[1, slot])

    group = min(4, n_z)

    def images(slot):
        def some(g, carry):
            xt, zt = g // (n_z // group), (g % (n_z // group)) * group
            lot = jnp.concatenate([dir_x[slot, xt, zt + i] for i in range(group)], axis=0)
            lot = lot.T
            for i in range(group):
                for u in range(2):
                    n = 2 * i + u
                    image = jnp.sum(gram[(xt * n_z + zt) * 2 + n] * lot[:, n:n + 1], axis=0, keepdims=True)
                    part[slot, xt, zt + i, pl.ds(u, 1), :] = image
            return carry

        lax.fori_loop(0, n_x * n_z // group, some, 0)

    right = reduce(ITERS)
    norm = jnp.sum(right * right, axis=-1, keepdims=True)

    def iterate(n, state):
        answer, residual, direction, norm = state
        gather(n, direction)
        images(n)
        image = reduce(n) + 0.1 * direction
        step = norm / jnp.sum(direction * image, axis=-1, keepdims=True)
        answer = answer + step * direction
        residual = residual - step * image
        after = jnp.sum(residual * residual, axis=-1, keepdims=True)
        direction = residual + (after / norm) * direction
        return answer, residual, direction, after

    state = lax.fori_loop(0, ITERS, iterate, (jnp.zeros_like(right), right, right, norm))
    out[...] = state[0]

    def sent(slot, carry):
        gathered_z(slot).wait_send()
        gathered_x(slot).wait_send()
        reduced_x(slot).wait_send()
        reduced_z(slot).wait_send()
        return carry

    lax.fori_loop(0, ITERS, sent, 0)
    reduced_x(ITERS).wait_send()
    reduced_z(ITERS).wait_send()


def body(n_x, n_z, ratings, confidence, rated, item_factors, cold_owner, cold_local, hot_group, hot_local):
    message, ids = prepare(n_x, n_z, ratings, confidence, rated, cold_owner, cold_local, hot_group)
    groups = lax.axis_index("dp") // 2 * 2 + jnp.arange(2, dtype=i32)
    hot_id = jnp.sum(jnp.where(hot_group[None, :] == groups[:, None], hot_local[None, :], 0), axis=1)
    users = confidence.shape[0]
    rows, width = item_factors.shape
    slots = ITERS + 1
    vmem = pl.BlockSpec(memory_space=pltpu.VMEM)
    smem = pl.BlockSpec(memory_space=pltpu.SMEM)
    dma = pltpu.SemaphoreType.DMA
    return pl.pallas_call(
        functools.partial(kernel, n_x, n_z),
        out_shape=jax.ShapeDtypeStruct((users, width), f32),
        in_specs=[vmem, vmem, pl.BlockSpec(memory_space=pl.ANY), smem],
        out_specs=vmem,
        scratch_shapes=[
            pltpu.VMEM((2, 4 * rows // BLK, BLK, width), bf16),
            pltpu.VMEM((n_z, n_x, 16, width), bf16),
            pltpu.VMEM((n_x, n_z, 16, width), bf16),
            pltpu.VMEM((n_z, n_x, 1, 128), i32),
            pltpu.VMEM((n_x, n_z, 1, 128), i32),
            pltpu.SMEM((n_x, n_z, 1, 128), i32),
            pltpu.VMEM((n_x * n_z * users, width, width), f32),
            pltpu.VMEM((slots, n_x, n_z, users, width), f32),
            pltpu.VMEM((slots, n_z, users, width), f32),
            pltpu.VMEM((slots, n_x, n_z, users, width), f32),
            pltpu.VMEM((slots, n_z, users, width), f32),
            pltpu.VMEM((slots, n_z, users, width), f32),
            pltpu.VMEM((slots, n_x, n_z, users, width), f32),
            dma((6,)), dma((6,)), dma((8,)), dma((8,)), dma((2,)),
            dma((2,)), dma((2,)), dma((2,)), dma((2,)),
            dma((2, slots)), dma((2, slots)), dma((2, slots)), dma((2, slots)),
        ],
        compiler_params=pltpu.CompilerParams(
            collective_id=0, has_side_effects=True, vmem_limit_bytes=40 * 1024 * 1024),
    )(message, ids, item_factors.reshape(-1, BLK, width), hot_id)


def solution(mesh):
    n_dp = mesh.shape["dp"]
    n_x = N_X
    n_z = n_dp // (2 * n_x)
    in_specs = (
        P(("dp", "rep"), None),
        P(("dp", "rep"), None),
        P(("dp", "rep"), None),
        P(("dp", "rep"), None),
        P("dp", "rep", None, None),
        P("dp", "rep", None),
        P(),
        P(),
    )
    return jax.shard_map(
        functools.partial(body, n_x, n_z), mesh=mesh, in_specs=in_specs,
        out_specs=P(("dp", "rep"), None), check_vma=False)
```

```python
import functools

import jax
import jax.numpy as jnp
from jax import lax
from jax.experimental import pallas as pl
from jax.experimental.pallas import tpu as pltpu
from jax.sharding import PartitionSpec as P

BLK = 64
CAP = 2
ITERS = 3
N_X = 4
MESH = pl.DeviceIdType.MESH
bf16, f32, i32 = jnp.bfloat16, jnp.float32, jnp.int32


def prepare(n_x, n_z, ratings, confidence, rated, cold_owner, cold_local, hot_group):
    pairs = n_x * n_z
    owners = cold_owner.reshape(-1)
    local_ids = cold_local.reshape(-1)
    cold = owners.shape[0]
    order = jnp.arange(cold, dtype=i32)
    same = (owners[:, None] == owners[None, :]) & (order[None, :] < order[:, None])
    slot_of = jnp.sum(same.astype(i32), axis=1)
    position = owners * CAP + slot_of
    match = position[None, :] == jnp.arange(2 * pairs * CAP, dtype=i32)[:, None]
    users = confidence.shape[0]
    weights = confidence.reshape(users, -1, BLK) * rated.astype(bf16)[:, :, None]
    both = jnp.concatenate([weights, ratings.reshape(users, -1, BLK)], axis=0)
    both = both.transpose(1, 0, 2).reshape(-1, 2 * users * BLK)
    cold_part = jnp.dot(match.astype(bf16), both[:cold], preferred_element_type=f32).astype(bf16)
    cold_part = cold_part.reshape(n_x, n_z, 2 * CAP, 2 * users, BLK).transpose(1, 0, 3, 2, 4)
    cold_part = cold_part.reshape(n_z, n_x, 2 * users, CAP, 2 * BLK)
    hot_match = hot_group[None, :] == jnp.arange(2 * pairs, dtype=i32)[:, None]
    hot_part = jnp.dot(hot_match.astype(bf16), both[cold:], preferred_element_type=f32).astype(bf16)
    hot_part = hot_part.reshape(n_x, n_z, 2, 2 * users, BLK).transpose(1, 0, 3, 2, 4)
    hot_part = hot_part.reshape(n_z, n_x, 2 * users, 1, 2 * BLK)
    message = jnp.concatenate([cold_part, hot_part], axis=3).reshape(n_z, n_x, 6 * users, 2 * BLK)
    message = jnp.pad(message, ((0, 0), (0, 0), (0, 16 - 6 * users), (0, 0)))
    ids = jnp.sum(jnp.where(match, local_ids[None, :], 0), axis=1)
    ids = ids.reshape(n_x, n_z, 1, 2 * CAP).transpose(1, 0, 2, 3)
    ids = jnp.pad(ids, ((0, 0), (0, 0), (0, 0), (0, 128 - 2 * CAP)))
    return message, ids


def kernel(n_x, n_z, message, ids, items, hot_id, out,
           table, msg_z, msg_x, ids_z, ids_x, ids_s, one, two, one_x_half, one_x, one_z_half, one_z,
           two_z_half, two_z, two_x_half, two_x,
           y_send, y_recv, c_send, c_recv, l_sem, a_send, a_recv, b_send, b_recv,
           one_x_sem, one_z_sem, two_z_sem, two_x_sem):
    dp = lax.axis_index("dp")
    y = lax.axis_index("rep")
    core = dp % 2
    z = (dp // 2) % n_z
    x = dp // (2 * n_z)
    n_y = 4

    def at(x_to, z_to):
        return ((x_to * n_z + z_to) * 2 + core, y)

    up, down, far = (y + 1) % n_y, (y + n_y - 1) % n_y, (y + 2) % n_y
    up_id, down_id, mate_id = (dp, up), (dp, down), (x * n_z * 2 + z * 2 + 1 - core, y)

    def remote(src, dst, send, recv, to):
        return pltpu.make_async_remote_copy(
            src_ref=src, dst_ref=dst, send_sem=send, recv_sem=recv, device_id=to, device_id_type=MESH)

    def each(count, body):
        for k in range(1, count):
            body(k)

    def others(ref, lead=()):
        index = lead + (pl.ds(0, ref.shape[len(lead)] - 1),)
        return ref.at[index]

    def waiter(ref, send, recv):
        return remote(ref, ref, send, recv, mate_id)

    barrier = pltpu.get_barrier_semaphore()
    for to in (up_id, down_id, mate_id):
        pl.semaphore_signal(barrier, inc=1, device_id=to, device_id_type=MESH)
    each(n_z, lambda k: pl.semaphore_signal(
        barrier, inc=1, device_id=at(x, (z + k) % n_z), device_id_type=MESH))
    each(n_x, lambda k: pl.semaphore_signal(
        barrier, inc=1, device_id=at((x + k) % n_x, z), device_id_type=MESH))
    pl.semaphore_wait(barrier, 3 + n_z - 1 + n_x - 1)

    held = items.shape[0]
    half = held // 2

    def rows(of_core, of_y, h):
        return table.at[of_core, pl.ds(of_y * held + h * half, half)]

    def own(h):
        return items.at[pl.ds(h * half, half)]

    def up_copy(k):
        if k < 2:
            return remote(own(k), rows(core, y, k), y_send.at[k], y_recv.at[k], up_id)
        return remote(rows(core, down, 0), rows(core, down, 0), y_send.at[2], y_recv.at[2], up_id)

    def down_copy(k):
        if k < 2:
            return remote(own(1 - k), rows(core, y, 1 - k), y_send.at[3 + k], y_recv.at[3 + k], down_id)
        return remote(rows(core, up, 1), rows(core, up, 1), y_send.at[5], y_recv.at[5], down_id)

    def from_down(k):
        ref = rows(core, down, k) if k < 2 else rows(core, far, 0)
        return remote(ref, ref, y_send.at[k], y_recv.at[k], up_id)

    def from_up(k):
        ref = rows(core, up, 1 - k) if k < 2 else rows(core, far, 1)
        return remote(ref, ref, y_send.at[3 + k], y_recv.at[3 + k], down_id)

    def mate_copy(n, src, of_y, h):
        return remote(src, rows(core, of_y, h), c_send.at[n], c_recv.at[n], mate_id)

    def from_mate(n, of_y, h):
        ref = rows(1 - core, of_y, h)
        return remote(ref, ref, c_send.at[n], c_recv.at[n], mate_id)

    for k in range(2):
        up_copy(k).start()
        down_copy(k).start()
    keep = pltpu.make_async_copy(items, table.at[core, pl.ds(y * held, held)], l_sem.at[0])
    keep.start()

    def start_z(k):
        to = (z + k) % n_z
        remote(message.at[to], msg_z.at[z], a_send.at[0], a_recv.at[0], at(x, to)).start()
        remote(ids.at[to], ids_z.at[z], a_send.at[1], a_recv.at[1], at(x, to)).start()

    def start_x(k):
        to = (x + k) % n_x
        remote(msg_z.at[:, to], msg_x.at[x], b_send.at[0], b_recv.at[0], at(to, z)).start()
        remote(ids_z.at[:, to], ids_x.at[x], b_send.at[1], b_recv.at[1], at(to, z)).start()

    z_done = [waiter(others(msg_z), a_send.at[0], a_recv.at[0]), waiter(others(ids_z), a_send.at[1], a_recv.at[1])]
    x_done = [waiter(others(msg_x), b_send.at[0], b_recv.at[0]), waiter(others(ids_x), b_send.at[1], b_recv.at[1])]

    each(n_z, start_z)
    for h in range(2):
        mate_copy(h, own(h), y, h).start()
    msg_z[z] = message[z]
    ids_z[z] = ids[z]

    from_down(0).wait_recv()
    up_copy(2).start()
    from_up(0).wait_recv()
    down_copy(2).start()
    mate_copy(2, rows(core, down, 0), down, 0).start()
    mate_copy(3, rows(core, up, 1), up, 1).start()

    for copy in z_done:
        copy.wait_recv()
    each(n_x, start_x)
    msg_x[x] = msg_z[:, x]
    ids_x[x] = ids_z[:, x]

    from_down(1).wait_recv()
    mate_copy(4, rows(core, down, 1), down, 1).start()
    from_up(1).wait_recv()
    mate_copy(5, rows(core, up, 0), up, 0).start()

    for copy in x_done:
        copy.wait_recv()
    to_smem = pltpu.make_async_copy(ids_x, ids_s, l_sem.at[1])
    to_smem.start()

    from_down(2).wait_recv()
    mate_copy(6, rows(core, far, 0), far, 0).start()
    from_up(2).wait_recv()
    mate_copy(7, rows(core, far, 1), far, 1).start()

    for copy in z_done + x_done:
        copy.wait_send()
    for k in range(3):
        up_copy(k).wait_send()
        down_copy(k).wait_send()
    halves = [(y, 0), (y, 1), (down, 0), (up, 1), (down, 1), (up, 0), (far, 0), (far, 1)]
    for n, (of_y, h) in enumerate(halves):
        mate_copy(n, rows(core, of_y, h), of_y, h).wait_send()
    for n, (of_y, h) in enumerate(halves):
        from_mate(n, of_y, h).wait_recv()
    keep.wait()
    to_smem.wait()

    hot_rows = [table[0, hot_id[0]], table[1, hot_id[1]]]
    row_of = lax.broadcasted_iota(i32, (16, 128), 0)
    masks = [((row_of == 6 + j) | (row_of == 9 + j)).astype(f32) for j in range(3)]
    lane_block = lax.broadcasted_iota(i32, (8, 128), 1) // 8
    window = [(lane_block >= i) & (lane_block < i + 8) for i in range(8)]

    def x_at(p):
        return (x + jnp.where(p == 0, 2, jnp.where(p == 1, 1, jnp.where(p == 2, 3, 0)))) % n_x

    def z_at(place):
        ahead = n_z // 2 - (place + 1) // 2
        behind = n_z // 2 + place // 2
        return (z + jnp.where(place % 2 == 1, ahead, behind)) % n_z

    def build(t, carry):
        p, place = t // n_z, t % n_z
        xt, zt = x_at(p), z_at(place)
        found = [table[s // CAP, ids_s[xt, zt, 0, s]] for s in range(2 * CAP)] + hot_rows
        chosen = jnp.concatenate(found, axis=0).T
        text = msg_x[xt, zt].astype(f32)
        scaled = []
        for u in range(2):
            weight = jnp.concatenate(
                [jnp.broadcast_to(text[3 * u + j:3 * u + j + 1], (128, 128)) for j in range(3)], axis=1)
            scaled.append(chosen * weight.astype(bf16))
        scaled = jnp.concatenate(scaled, axis=0)
        rating = jnp.concatenate([(text * masks[j]).astype(bf16) for j in range(3)], axis=1)
        left = jnp.concatenate([chosen, rating], axis=0)
        both = lax.dot_general(left, scaled, (((1,), (1,)), ((), ())), preferred_element_type=f32)

        def group(u, i):
            return both[8 * i:8 * i + 8, 128 * u:128 * u + 128]

        main = [[jnp.where(window[i], group(u, i), group(u, i + 8)) for i in range(8)] for u in range(2)]
        shared = group(0, 0)
        for i in range(8):
            shared = jnp.where(lane_block == i + 8, group(0, i), shared)
            shared = jnp.where(lane_block == i, group(1, i + 8), shared)
        right = [
            jnp.sum(both[134 + 3 * u:137 + 3 * u, 128 * u:128 * u + 128], axis=0, keepdims=True)
            for u in range(2)
        ]
        one[p, place] = jnp.concatenate(main[0], axis=0)
        two[p, place] = jnp.concatenate(main[1] + [shared] + right + [jnp.zeros((6, 128), f32)], axis=0)
        return carry

    lax.fori_loop(0, n_x * n_z, build, 0)

    last_x, last_z = n_x - 1, n_z - 1
    to_x = (at((x + 1) % n_x, z), at((x + n_x - 1) % n_x, z))
    to_z = (at(x, (z + 1) % n_z), at(x, (z + n_z - 1) % n_z))
    quarter = n_z // 4
    one_rows, two_rows = one.shape[2] // 2, two.shape[2] // 2
    steps_x, steps_z = n_x // 2, n_z // 2

    def place(way, step, steps):
        if step == steps:
            return 2 * steps - 1
        return 0 if step == 0 else 2 * step - 1 + way

    def one_x_copy(way, step, j):
        lots = pl.ds(quarter * j, quarter)
        sems = one_x_sem.at[0, way, step, j], one_x_sem.at[1, way, step, j]
        if step == 0:
            return remote(one.at[0, lots, pl.ds(one_rows * way, one_rows)], one_x_half.at[way, lots], *sems, to_x[way])
        return remote(one.at[place(way, step, steps_x), lots], one_x.at[way, step - 1, lots], *sems, to_x[way])

    def one_z_copy(way, step):
        sems = one_z_sem.at[0, way, step], one_z_sem.at[1, way, step]
        if step == 0:
            return remote(one.at[last_x, 0, pl.ds(one_rows * way, one_rows)], one_z_half.at[way], *sems, to_z[way])
        return remote(one.at[last_x, place(way, step, steps_z)], one_z.at[way, step - 1], *sems, to_z[way])

    def two_z_copy(way, step, p):
        sems = two_z_sem.at[0, way, step, p], two_z_sem.at[1, way, step, p]
        if step == 0:
            return remote(two.at[p, 0, pl.ds(two_rows * way, two_rows)], two_z_half.at[way, p], *sems, to_z[way])
        return remote(two.at[p, place(way, step, steps_z)], two_z.at[way, step - 1, p], *sems, to_z[way])

    def two_x_copy(way, step):
        sems = two_x_sem.at[0, way, step], two_x_sem.at[1, way, step]
        if step == 0:
            return remote(two.at[0, last_z, pl.ds(two_rows * way, two_rows)], two_x_half.at[way], *sems, to_x[way])
        return remote(two.at[place(way, step, steps_x), last_z], two_x.at[way, step - 1], *sems, to_x[way])

    def one_x_event(step, j):
        for way in range(2):
            one_x_copy(way, step, j).wait_recv()
            lots = pl.ds(quarter * j, quarter)
            at_place = place(way, step + 1, steps_x)
            if step == 0:
                one[at_place, lots, pl.ds(one_rows * way, one_rows)] += one_x_half[way, lots]
            else:
                one[at_place, lots] += one_x[way, step - 1, lots]
            if step + 1 < steps_x:
                one_x_copy(way, step + 1, j).start()

    def one_z_event(step):
        for way in range(2):
            one_z_copy(way, step).wait_recv()
            at_place = place(way, step + 1, steps_z)
            if step == 0:
                one[last_x, at_place, pl.ds(one_rows * way, one_rows)] += one_z_half[way]
            else:
                one[last_x, at_place] += one_z[way, step - 1]
            if step + 1 < steps_z:
                one_z_copy(way, step + 1).start()

    def two_z_event(step, p):
        for way in range(2):
            two_z_copy(way, step, p).wait_recv()
            at_place = place(way, step + 1, steps_z)
            if step == 0:
                two[p, at_place, pl.ds(two_rows * way, two_rows)] += two_z_half[way, p]
            else:
                two[p, at_place] += two_z[way, step - 1, p]
            if step + 1 < steps_z:
                two_z_copy(way, step + 1, p).start()

    def two_x_event(step):
        for way in range(2):
            two_x_copy(way, step).wait_recv()
            at_place = place(way, step + 1, steps_x)
            if step == 0:
                two[at_place, last_z, pl.ds(two_rows * way, two_rows)] += two_x_half[way]
            else:
                two[at_place, last_z] += two_x[way, step - 1]
            if step + 1 < steps_x:
                two_x_copy(way, step + 1).start()

    delay = 2.5
    one_unit, two_unit = 2.6, 0.82
    events = []
    for step in range(steps_x):
        for j in range(4):
            begun = 4 * one_unit * (step - 0.5) if step else 0.0
            events.append((delay + begun + one_unit * (j + 1) * (1 if step else 0.5), one_x_event, (step, j)))
    ready = [when for when, _, args in events if args[0] == steps_x - 1]

    def one_z_first():
        for way in range(2):
            one_z_copy(way, 0).start()

    def two_x_first():
        for way in range(2):
            two_x_copy(way, 0).start()

    when = ready[0] + 0.01
    events.append((when, one_z_first, ()))
    for step in range(steps_z):
        needed = max(place(way, step + 1, steps_z) for way in range(2)) // quarter
        when = max(when + 3.0, ready[needed] + 0.02)
        events.append((when, one_z_event, (step,)))
    for step in range(steps_z):
        for p in range(n_x):
            begun = 4 * two_unit * (step - 0.5) if step else 0.0
            when = delay + begun + two_unit * (p + 1) * (1 if step else 0.5)
            events.append((when, two_z_event, (step, p)))
    when += 0.01
    events.append((when, two_x_first, ()))
    for step in range(steps_x):
        when += 3.0
        events.append((when, two_x_event, (step,)))

    for j in range(4):
        for way in range(2):
            one_x_copy(way, 0, j).start()
            two_z_copy(way, 0, j).start()
    for _, event, args in sorted(events, key=lambda entry: entry[0]):
        event(*args)

    row_block = lax.broadcasted_iota(i32, (128, 128), 0) // 8
    own_block = row_block == lax.broadcasted_iota(i32, (128, 128), 1) // 8
    lot = two[last_x, last_z]
    grams = []
    for u in range(2):
        main = one[last_x, last_z] if u == 0 else lot[:64]
        upper = [jnp.where(window[i], main[8 * i:8 * i + 8], 0.0) for i in range(8)]
        lower = [jnp.where(window[i], 0.0, main[8 * i:8 * i + 8]) for i in range(8)]
        for i in range(8):
            if u == 0:
                upper[i] = jnp.where(lane_block == i + 8, lot[64:72], upper[i])
            else:
                lower[i] = jnp.where(lane_block == i, lot[64:72], lower[i])
        kept = jnp.concatenate(upper + lower, axis=0)
        grams.append(kept + jnp.where(own_block, 0.0, kept).T)
    right = lot[72:74]

    def iterate(n, state):
        answer, residual, direction, norm = state
        turned = jnp.concatenate([direction, jnp.zeros((6, 128), f32)], axis=0).T
        image = jnp.concatenate(
            [jnp.sum(grams[u] * turned[:, u:u + 1], axis=0, keepdims=True) for u in range(2)], axis=0)
        image = image + 0.1 * direction
        step = norm / jnp.sum(direction * image, axis=-1, keepdims=True)
        answer = answer + step * direction
        residual = residual - step * image
        after = jnp.sum(residual * residual, axis=-1, keepdims=True)
        direction = residual + (after / norm) * direction
        return answer, residual, direction, after

    state = (jnp.zeros_like(right), right, right, jnp.sum(right * right, axis=-1, keepdims=True))
    for n in range(ITERS):
        state = iterate(n, state)
    out[...] = state[0]

    for way in range(2):
        for step in range(steps_x):
            two_x_copy(way, step).wait_send()
            for j in range(4):
                one_x_copy(way, step, j).wait_send()
        for step in range(steps_z):
            one_z_copy(way, step).wait_send()
            for p in range(n_x):
                two_z_copy(way, step, p).wait_send()


def body(n_x, n_z, ratings, confidence, rated, item_factors, cold_owner, cold_local, hot_group, hot_local):
    message, ids = prepare(n_x, n_z, ratings, confidence, rated, cold_owner, cold_local, hot_group)
    groups = lax.axis_index("dp") // 2 * 2 + jnp.arange(2, dtype=i32)
    hot_id = jnp.sum(jnp.where(hot_group[None, :] == groups[:, None], hot_local[None, :], 0), axis=1)
    users = confidence.shape[0]
    rows, width = item_factors.shape
    vmem = pl.BlockSpec(memory_space=pltpu.VMEM)
    smem = pl.BlockSpec(memory_space=pltpu.SMEM)
    dma = pltpu.SemaphoreType.DMA
    return pl.pallas_call(
        functools.partial(kernel, n_x, n_z),
        out_shape=jax.ShapeDtypeStruct((users, width), f32),
        in_specs=[vmem, vmem, pl.BlockSpec(memory_space=pl.ANY), smem],
        out_specs=vmem,
        scratch_shapes=[
            pltpu.VMEM((2, 4 * rows // BLK, BLK, width), bf16),
            pltpu.VMEM((n_z, n_x, 16, width), bf16),
            pltpu.VMEM((n_x, n_z, 16, width), bf16),
            pltpu.VMEM((n_z, n_x, 1, 128), i32),
            pltpu.VMEM((n_x, n_z, 1, 128), i32),
            pltpu.SMEM((n_x, n_z, 1, 128), i32),
            pltpu.VMEM((n_x, n_z, 64, width), f32),
            pltpu.VMEM((n_x, n_z, 80, width), f32),
            pltpu.VMEM((2, n_z, 32, width), f32),
            pltpu.VMEM((2, n_x // 2 - 1, n_z, 64, width), f32),
            pltpu.VMEM((2, 32, width), f32),
            pltpu.VMEM((2, n_z // 2 - 1, 64, width), f32),
            pltpu.VMEM((2, n_x, 40, width), f32),
            pltpu.VMEM((2, n_z // 2 - 1, n_x, 80, width), f32),
            pltpu.VMEM((2, 40, width), f32),
            pltpu.VMEM((2, n_x // 2 - 1, 80, width), f32),
            dma((6,)), dma((6,)), dma((8,)), dma((8,)), dma((2,)),
            dma((2,)), dma((2,)), dma((2,)), dma((2,)),
            dma((2, 2, n_x // 2, 4)), dma((2, 2, n_z // 2)), dma((2, 2, n_z // 2, n_x)), dma((2, 2, n_x // 2)),
        ],
        compiler_params=pltpu.CompilerParams(
            collective_id=0, has_side_effects=True, vmem_limit_bytes=40 * 1024 * 1024),
    )(message, ids, item_factors.reshape(-1, BLK, width), hot_id)


def solution(mesh):
    n_dp = mesh.shape["dp"]
    n_x = N_X
    n_z = n_dp // (2 * n_x)
    in_specs = (
        P(("dp", "rep"), None),
        P(("dp", "rep"), None),
        P(("dp", "rep"), None),
        P(("dp", "rep"), None),
        P("dp", "rep", None, None),
        P("dp", "rep", None),
        P(),
        P(),
    )
    return jax.shard_map(
        functools.partial(body, n_x, n_z), mesh=mesh, in_specs=in_specs,
        out_specs=P(("dp", "rep"), None), check_vma=False)
```

```python
import functools

import jax
import jax.numpy as jnp
from jax import lax
from jax.experimental import pallas as pl
from jax.experimental.pallas import tpu as pltpu
from jax.sharding import PartitionSpec as P

BLK = 64
CAP = 2
ITERS = 3
N_X = 4
PACKED_ROWS = 144
ONE_ROWS = 80
TWO_ROWS = PACKED_ROWS - ONE_ROWS
LOTS_X = 4
LOTS_Z = 4
MESH = pl.DeviceIdType.MESH
bf16, f32, i32 = jnp.bfloat16, jnp.float32, jnp.int32


def prepare(n_x, n_z, ratings, confidence, rated, cold_owner, cold_local, hot_group):
    pairs = n_x * n_z
    owners = cold_owner.reshape(-1)
    local_ids = cold_local.reshape(-1)
    cold = owners.shape[0]
    order = jnp.arange(cold, dtype=i32)
    same = (owners[:, None] == owners[None, :]) & (order[None, :] < order[:, None])
    slot_of = jnp.sum(same.astype(i32), axis=1)
    position = owners * CAP + slot_of
    match = position[None, :] == jnp.arange(2 * pairs * CAP, dtype=i32)[:, None]
    users = confidence.shape[0]
    weights = confidence.reshape(users, -1, BLK) * rated.astype(bf16)[:, :, None]
    both = jnp.concatenate([weights, ratings.reshape(users, -1, BLK)], axis=0)
    both = both.transpose(1, 0, 2).reshape(-1, 2 * users * BLK)
    cold_part = jnp.dot(match.astype(bf16), both[:cold], preferred_element_type=f32).astype(bf16)
    cold_part = cold_part.reshape(n_x, n_z, 2 * CAP, 2 * users, BLK).transpose(1, 0, 3, 2, 4)
    cold_part = cold_part.reshape(n_z, n_x, 2 * users, CAP, 2 * BLK)
    hot_match = hot_group[None, :] == jnp.arange(2 * pairs, dtype=i32)[:, None]
    hot_part = jnp.dot(hot_match.astype(bf16), both[cold:], preferred_element_type=f32).astype(bf16)
    hot_part = hot_part.reshape(n_x, n_z, 2, 2 * users, BLK).transpose(1, 0, 3, 2, 4)
    hot_part = hot_part.reshape(n_z, n_x, 2 * users, 1, 2 * BLK)
    message = jnp.concatenate([cold_part, hot_part], axis=3).reshape(n_z, n_x, 6 * users, 2 * BLK)
    message = jnp.pad(message, ((0, 0), (0, 0), (0, 16 - 6 * users), (0, 0)))
    ids = jnp.sum(jnp.where(match, local_ids[None, :], 0), axis=1)
    ids = ids.reshape(n_x, n_z, 1, 2 * CAP).transpose(1, 0, 2, 3)
    ids = jnp.pad(ids, ((0, 0), (0, 0), (0, 0), (0, 128 - 2 * CAP)))
    return message, ids


def kernel(n_x, n_z, message, ids, items, hot_id, out,
           table, msg_z, msg_x, ids_z, ids_x, ids_s, one, two, one_x_half, one_x, one_z_half, one_z,
           two_z_half, two_z, two_x_half, two_x,
           y_send, y_recv, c_send, c_recv, l_sem, a_send, a_recv, b_send, b_recv,
           one_x_sem, one_z_sem, two_z_sem, two_x_sem):
    dp = lax.axis_index("dp")
    y = lax.axis_index("rep")
    core = dp % 2
    z = (dp // 2) % n_z
    x = dp // (2 * n_z)
    n_y = 4

    def at(x_to, z_to):
        return ((x_to * n_z + z_to) * 2 + core, y)

    up, down, far = (y + 1) % n_y, (y + n_y - 1) % n_y, (y + 2) % n_y
    up_id, down_id, mate_id = (dp, up), (dp, down), (x * n_z * 2 + z * 2 + 1 - core, y)

    def remote(src, dst, send, recv, to):
        return pltpu.make_async_remote_copy(
            src_ref=src, dst_ref=dst, send_sem=send, recv_sem=recv, device_id=to, device_id_type=MESH)

    def each(count, body):
        for k in range(1, count):
            body(k)

    def others(ref, lead=()):
        index = lead + (pl.ds(0, ref.shape[len(lead)] - 1),)
        return ref.at[index]

    def waiter(ref, send, recv):
        return remote(ref, ref, send, recv, mate_id)

    barrier = pltpu.get_barrier_semaphore()
    for to in (up_id, down_id, mate_id):
        pl.semaphore_signal(barrier, inc=1, device_id=to, device_id_type=MESH)
    each(n_z, lambda k: pl.semaphore_signal(
        barrier, inc=1, device_id=at(x, (z + k) % n_z), device_id_type=MESH))
    each(n_x, lambda k: pl.semaphore_signal(
        barrier, inc=1, device_id=at((x + k) % n_x, z), device_id_type=MESH))
    pl.semaphore_wait(barrier, 3 + n_z - 1 + n_x - 1)

    held = items.shape[0]
    half = held // 2

    def rows(of_core, of_y, h):
        return table.at[of_core, pl.ds(of_y * held + h * half, half)]

    def own(h):
        return items.at[pl.ds(h * half, half)]

    def up_copy(k):
        if k < 2:
            return remote(own(k), rows(core, y, k), y_send.at[k], y_recv.at[k], up_id)
        return remote(rows(core, down, 0), rows(core, down, 0), y_send.at[2], y_recv.at[2], up_id)

    def down_copy(k):
        if k < 2:
            return remote(own(1 - k), rows(core, y, 1 - k), y_send.at[3 + k], y_recv.at[3 + k], down_id)
        return remote(rows(core, up, 1), rows(core, up, 1), y_send.at[5], y_recv.at[5], down_id)

    def from_down(k):
        ref = rows(core, down, k) if k < 2 else rows(core, far, 0)
        return remote(ref, ref, y_send.at[k], y_recv.at[k], up_id)

    def from_up(k):
        ref = rows(core, up, 1 - k) if k < 2 else rows(core, far, 1)
        return remote(ref, ref, y_send.at[3 + k], y_recv.at[3 + k], down_id)

    def mate_copy(n, src, of_y, h):
        return remote(src, rows(core, of_y, h), c_send.at[n], c_recv.at[n], mate_id)

    def from_mate(n, of_y, h):
        ref = rows(1 - core, of_y, h)
        return remote(ref, ref, c_send.at[n], c_recv.at[n], mate_id)

    for k in range(2):
        up_copy(k).start()
        down_copy(k).start()
    keep = pltpu.make_async_copy(items, table.at[core, pl.ds(y * held, held)], l_sem.at[0])
    keep.start()

    def start_z(k):
        to = (z + k) % n_z
        remote(message.at[to], msg_z.at[z], a_send.at[0], a_recv.at[0], at(x, to)).start()
        remote(ids.at[to], ids_z.at[z], a_send.at[1], a_recv.at[1], at(x, to)).start()

    def start_x(k):
        to = (x + k) % n_x
        remote(msg_z.at[:, to], msg_x.at[x], b_send.at[0], b_recv.at[0], at(to, z)).start()
        remote(ids_z.at[:, to], ids_x.at[x], b_send.at[1], b_recv.at[1], at(to, z)).start()

    z_done = [waiter(others(msg_z), a_send.at[0], a_recv.at[0]), waiter(others(ids_z), a_send.at[1], a_recv.at[1])]
    x_done = [waiter(others(msg_x), b_send.at[0], b_recv.at[0]), waiter(others(ids_x), b_send.at[1], b_recv.at[1])]

    each(n_z, start_z)
    for h in range(2):
        mate_copy(h, own(h), y, h).start()
    msg_z[z] = message[z]
    ids_z[z] = ids[z]

    from_down(0).wait_recv()
    up_copy(2).start()
    from_up(0).wait_recv()
    down_copy(2).start()
    mate_copy(2, rows(core, down, 0), down, 0).start()
    mate_copy(3, rows(core, up, 1), up, 1).start()

    for copy in z_done:
        copy.wait_recv()
    each(n_x, start_x)
    msg_x[x] = msg_z[:, x]
    ids_x[x] = ids_z[:, x]

    from_down(1).wait_recv()
    mate_copy(4, rows(core, down, 1), down, 1).start()
    from_up(1).wait_recv()
    mate_copy(5, rows(core, up, 0), up, 0).start()

    for copy in x_done:
        copy.wait_recv()
    to_smem = pltpu.make_async_copy(ids_x, ids_s, l_sem.at[1])
    to_smem.start()

    from_down(2).wait_recv()
    mate_copy(6, rows(core, far, 0), far, 0).start()
    from_up(2).wait_recv()
    mate_copy(7, rows(core, far, 1), far, 1).start()

    for copy in z_done + x_done:
        copy.wait_send()
    for k in range(3):
        up_copy(k).wait_send()
        down_copy(k).wait_send()
    halves = [(y, 0), (y, 1), (down, 0), (up, 1), (down, 1), (up, 0), (far, 0), (far, 1)]
    for n, (of_y, h) in enumerate(halves):
        mate_copy(n, rows(core, of_y, h), of_y, h).wait_send()
    for n, (of_y, h) in enumerate(halves):
        from_mate(n, of_y, h).wait_recv()
    keep.wait()
    to_smem.wait()

    hot_rows = [table[0, hot_id[0]], table[1, hot_id[1]]]
    row_of = lax.broadcasted_iota(i32, (16, 128), 0)
    masks = [((row_of == 6 + j) | (row_of == 9 + j)).astype(f32) for j in range(3)]
    lane_block = lax.broadcasted_iota(i32, (8, 128), 1) // 8
    window = [(lane_block >= i) & (lane_block < i + 8) for i in range(8)]

    def z_at(place):
        ahead = n_z // 2 - (place + 1) // 2
        behind = n_z // 2 + place // 2
        return (z + jnp.where(place % 2 == 1, ahead, behind)) % n_z

    def build(place, carry):
        for p in range(n_x):
            build_one(p, place)
        return carry

    def build_one(p, place):
        xt, zt = (x + (2, 1, 3, 0)[p]) % n_x, z_at(place)
        found = [table[s // CAP, ids_s[xt, zt, 0, s]] for s in range(2 * CAP)] + hot_rows
        chosen = jnp.concatenate(found, axis=0).T
        text = msg_x[xt, zt].astype(f32)
        scaled = []
        for u in range(2):
            weight = jnp.concatenate(
                [jnp.broadcast_to(text[3 * u + j:3 * u + j + 1], (128, 128)) for j in range(3)], axis=1)
            scaled.append(chosen * weight.astype(bf16))
        scaled = jnp.concatenate(scaled, axis=0)
        rating = jnp.concatenate([(text * masks[j]).astype(bf16) for j in range(3)], axis=1)
        left = jnp.concatenate([chosen, rating], axis=0)
        both = lax.dot_general(left, scaled, (((1,), (1,)), ((), ())), preferred_element_type=f32)

        def group(u, i):
            return both[8 * i:8 * i + 8, 128 * u:128 * u + 128]

        main = [[jnp.where(window[i], group(u, i), group(u, i + 8)) for i in range(8)] for u in range(2)]
        shared = group(0, 0)
        for i in range(8):
            shared = jnp.where(lane_block == i + 8, group(0, i), shared)
            shared = jnp.where(lane_block == i, group(1, i + 8), shared)
        right = [
            jnp.sum(both[134 + 3 * u:137 + 3 * u, 128 * u:128 * u + 128], axis=0, keepdims=True)
            for u in range(2)
        ]
        packed = main[0] + main[1] + [shared, jnp.concatenate(right + [jnp.zeros((6, 128), f32)], axis=0)]
        one[p, place] = jnp.concatenate(packed[:one.shape[2] // 8], axis=0)
        two[p, place] = jnp.concatenate(packed[one.shape[2] // 8:], axis=0)

    last_x, last_z = n_x - 1, n_z - 1
    to_x = (at((x + 1) % n_x, z), at((x + n_x - 1) % n_x, z))
    to_z = (at(x, (z + 1) % n_z), at(x, (z + n_z - 1) % n_z))
    quarter = n_z // LOTS_X
    wide = n_x // LOTS_Z
    one_rows, two_rows = one.shape[2] // 2, two.shape[2] // 2
    steps_x, steps_z = n_x // 2, n_z // 2

    def place(way, step, steps):
        if step == steps:
            return 2 * steps - 1
        return 0 if step == 0 else 2 * step - 1 + way

    def one_x_copy(way, step, j):
        lots = pl.ds(quarter * j, quarter)
        sems = one_x_sem.at[0, way, step, j], one_x_sem.at[1, way, step, j]
        if step == 0:
            return remote(one.at[0, lots, pl.ds(one_rows * way, one_rows)], one_x_half.at[way, lots], *sems, to_x[way])
        return remote(one.at[place(way, step, steps_x), lots], one_x.at[way, step - 1, lots], *sems, to_x[way])

    def one_z_copy(way, step):
        sems = one_z_sem.at[0, way, step], one_z_sem.at[1, way, step]
        if step == 0:
            return remote(one.at[last_x, 0, pl.ds(one_rows * way, one_rows)], one_z_half.at[way], *sems, to_z[way])
        return remote(one.at[last_x, place(way, step, steps_z)], one_z.at[way, step - 1], *sems, to_z[way])

    def two_z_copy(way, step, p):
        sems = two_z_sem.at[0, way, step, p], two_z_sem.at[1, way, step, p]
        lot = pl.ds(p * wide, wide)
        if step == 0:
            return remote(two.at[lot, 0, pl.ds(two_rows * way, two_rows)], two_z_half.at[way, lot], *sems, to_z[way])
        return remote(two.at[lot, place(way, step, steps_z)], two_z.at[way, step - 1, lot], *sems, to_z[way])

    def two_x_copy(way, step):
        sems = two_x_sem.at[0, way, step], two_x_sem.at[1, way, step]
        if step == 0:
            return remote(two.at[0, last_z, pl.ds(two_rows * way, two_rows)], two_x_half.at[way], *sems, to_x[way])
        return remote(two.at[place(way, step, steps_x), last_z], two_x.at[way, step - 1], *sems, to_x[way])

    delay, event_us, build_us = 2.5, 0.15, 0.5
    clock = {"now": 0.0, "x": 0.0, "z": 0.0}
    built, serial, pending, done_x, done_z = [0], [0], [], [], []

    def sent(axis, rows_sent, event, args):
        clock[axis] = max(clock[axis], clock["now"]) + rows_sent * 2 * 512 / 1e5
        serial[0] += 1
        pending.append((clock[axis] + delay, serial[0], event, args))

    def start_one_x(step, j):
        for way in range(2):
            one_x_copy(way, step, j).start()
        sent("x", quarter * one_rows * (2 if step else 1), one_x_event, (step, j))

    def start_one_z(step):
        for way in range(2):
            one_z_copy(way, step).start()
        sent("z", one_rows * (2 if step else 1), one_z_event, (step,))

    def start_two_z(step, p):
        for way in range(2):
            two_z_copy(way, step, p).start()
        sent("z", wide * two_rows * (2 if step else 1), two_z_event, (step, p))

    def start_two_x(step):
        for way in range(2):
            two_x_copy(way, step).start()
        sent("x", two_rows * (2 if step else 1), two_x_event, (step,))

    def ready_one_z():
        step = len(done_z)
        needed = max(place(way, step, steps_z) for way in range(2)) // quarter
        if step < steps_z and needed in done_x and ("one", step) not in begun:
            begun.add(("one", step))
            start_one_z(step)

    begun = set()

    def one_x_event(step, j):
        for way in range(2):
            one_x_copy(way, step, j).wait()
            lots = pl.ds(quarter * j, quarter)
            at_place = place(way, step + 1, steps_x)
            if step == 0:
                one[at_place, lots, pl.ds(one_rows * way, one_rows)] += one_x_half[way, lots]
            else:
                one[at_place, lots] += one_x[way, step - 1, lots]
        if step + 1 < steps_x:
            start_one_x(step + 1, j)
        else:
            done_x.append(j)
            ready_one_z()

    def one_z_event(step):
        for way in range(2):
            one_z_copy(way, step).wait()
            at_place = place(way, step + 1, steps_z)
            if step == 0:
                one[last_x, at_place, pl.ds(one_rows * way, one_rows)] += one_z_half[way]
            else:
                one[last_x, at_place] += one_z[way, step - 1]
        done_z.append(step)
        ready_one_z()

    def two_z_event(step, p):
        lot = pl.ds(p * wide, wide)
        for way in range(2):
            two_z_copy(way, step, p).wait()
            at_place = place(way, step + 1, steps_z)
            while at_place >= built[0]:
                build_some()
            if step == 0:
                two[lot, at_place, pl.ds(two_rows * way, two_rows)] += two_z_half[way, lot]
            else:
                two[lot, at_place] += two_z[way, step - 1, lot]
        if step + 1 < steps_z:
            start_two_z(step + 1, p)
        elif p == n_x // wide - 1:
            start_two_x(0)

    def two_x_event(step):
        for way in range(2):
            two_x_copy(way, step).wait()
            at_place = place(way, step + 1, steps_x)
            if step == 0:
                two[at_place, last_z, pl.ds(two_rows * way, two_rows)] += two_x_half[way]
            else:
                two[at_place, last_z] += two_x[way, step - 1]
        if step + 1 < steps_x:
            start_two_x(step + 1)

    def build_some():
        first = built[0]
        size = 1 if first == 0 else n_z // 4 - first % (n_z // 4)
        lax.fori_loop(first, first + size, build, 0)
        built[0] += size
        clock["now"] += build_us * size
        if first == 0:
            for p in range(n_x // wide):
                start_two_z(0, p)
        if built[0] % quarter == 0:
            start_one_x(0, built[0] // quarter - 1)

    while pending or built[0] < n_z:
        pending.sort()
        if built[0] < n_z and not (pending and pending[0][0] <= clock["now"]):
            build_some()
            continue
        arrival, _, event, args = pending.pop(0)
        clock["now"] = max(clock["now"], arrival) + event_us
        event(*args)

    row_block = lax.broadcasted_iota(i32, (128, 128), 0) // 8
    own_block = row_block == lax.broadcasted_iota(i32, (128, 128), 1) // 8
    lot = jnp.concatenate([one[last_x, last_z], two[last_x, last_z]], axis=0)
    grams = []
    for u in range(2):
        main = lot[64 * u:64 * u + 64]
        upper = [jnp.where(window[i], main[8 * i:8 * i + 8], 0.0) for i in range(8)]
        lower = [jnp.where(window[i], 0.0, main[8 * i:8 * i + 8]) for i in range(8)]
        for i in range(8):
            if u == 0:
                upper[i] = jnp.where(lane_block == i + 8, lot[128:136], upper[i])
            else:
                lower[i] = jnp.where(lane_block == i, lot[128:136], lower[i])
        kept = jnp.concatenate(upper + lower, axis=0)
        grams.append(kept + jnp.where(own_block, 0.0, kept).T)
    right = lot[136:138]

    def iterate(n, state):
        answer, residual, direction, norm = state
        turned = jnp.concatenate([direction, jnp.zeros((6, 128), f32)], axis=0).T
        image = jnp.concatenate(
            [jnp.sum(grams[u] * turned[:, u:u + 1], axis=0, keepdims=True) for u in range(2)], axis=0)
        image = image + 0.1 * direction
        step = norm / jnp.sum(direction * image, axis=-1, keepdims=True)
        answer = answer + step * direction
        residual = residual - step * image
        after = jnp.sum(residual * residual, axis=-1, keepdims=True)
        direction = residual + (after / norm) * direction
        return answer, residual, direction, after

    state = (jnp.zeros_like(right), right, right, jnp.sum(right * right, axis=-1, keepdims=True))
    for n in range(ITERS):
        state = iterate(n, state)
    out[...] = state[0]


def body(n_x, n_z, ratings, confidence, rated, item_factors, cold_owner, cold_local, hot_group, hot_local):
    message, ids = prepare(n_x, n_z, ratings, confidence, rated, cold_owner, cold_local, hot_group)
    groups = lax.axis_index("dp") // 2 * 2 + jnp.arange(2, dtype=i32)
    hot_id = jnp.sum(jnp.where(hot_group[None, :] == groups[:, None], hot_local[None, :], 0), axis=1)
    users = confidence.shape[0]
    rows, width = item_factors.shape
    vmem = pl.BlockSpec(memory_space=pltpu.VMEM)
    smem = pl.BlockSpec(memory_space=pltpu.SMEM)
    dma = pltpu.SemaphoreType.DMA
    return pl.pallas_call(
        functools.partial(kernel, n_x, n_z),
        out_shape=jax.ShapeDtypeStruct((users, width), f32),
        in_specs=[vmem, vmem, pl.BlockSpec(memory_space=pl.ANY), smem],
        out_specs=vmem,
        scratch_shapes=[
            pltpu.VMEM((2, 4 * rows // BLK, BLK, width), bf16),
            pltpu.VMEM((n_z, n_x, 16, width), bf16),
            pltpu.VMEM((n_x, n_z, 16, width), bf16),
            pltpu.VMEM((n_z, n_x, 1, 128), i32),
            pltpu.VMEM((n_x, n_z, 1, 128), i32),
            pltpu.SMEM((n_x, n_z, 1, 128), i32),
            pltpu.VMEM((n_x, n_z, ONE_ROWS, width), f32),
            pltpu.VMEM((n_x, n_z, TWO_ROWS, width), f32),
            pltpu.VMEM((2, n_z, ONE_ROWS // 2, width), f32),
            pltpu.VMEM((2, n_x // 2 - 1, n_z, ONE_ROWS, width), f32),
            pltpu.VMEM((2, ONE_ROWS // 2, width), f32),
            pltpu.VMEM((2, n_z // 2 - 1, ONE_ROWS, width), f32),
            pltpu.VMEM((2, n_x, TWO_ROWS // 2, width), f32),
            pltpu.VMEM((2, n_z // 2 - 1, n_x, TWO_ROWS, width), f32),
            pltpu.VMEM((2, TWO_ROWS // 2, width), f32),
            pltpu.VMEM((2, n_x // 2 - 1, TWO_ROWS, width), f32),
            dma((6,)), dma((6,)), dma((8,)), dma((8,)), dma((2,)),
            dma((2,)), dma((2,)), dma((2,)), dma((2,)),
            dma((2, 2, n_x // 2, LOTS_X)), dma((2, 2, n_z // 2)), dma((2, 2, n_z // 2, LOTS_Z)), dma((2, 2, n_x // 2)),
        ],
        compiler_params=pltpu.CompilerParams(
            collective_id=0, has_side_effects=True, vmem_limit_bytes=40 * 1024 * 1024),
    )(message, ids, item_factors.reshape(-1, BLK, width), hot_id)


def solution(mesh):
    n_dp = mesh.shape["dp"]
    n_x = N_X
    n_z = n_dp // (2 * n_x)
    in_specs = (
        P(("dp", "rep"), None),
        P(("dp", "rep"), None),
        P(("dp", "rep"), None),
        P(("dp", "rep"), None),
        P("dp", "rep", None, None),
        P("dp", "rep", None),
        P(),
        P(),
    )
    return jax.shard_map(
        functools.partial(body, n_x, n_z), mesh=mesh, in_specs=in_specs,
        out_specs=P(("dp", "rep"), None), check_vma=False)
```

```python
import functools

import jax
import jax.numpy as jnp
from jax import lax
from jax.experimental import pallas as pl
from jax.experimental.pallas import tpu as pltpu
from jax.sharding import PartitionSpec as P

BLK = 64
CAP = 2
ITERS = 3
N_X = 4
PACKED_ROWS = 144
ONE_ROWS = 80
TWO_ROWS = PACKED_ROWS - ONE_ROWS
X_CUTS = (0, 1, 3, 5, 7, 11)
LOTS_Z = 4
MESH = pl.DeviceIdType.MESH
bf16, f32, i32 = jnp.bfloat16, jnp.float32, jnp.int32


def blocks_of(values):
    users = values.shape[0]
    values = values.reshape(users, -1, BLK)
    return jnp.pad(values, ((0, 0), (0, -values.shape[1] % 128), (0, 0)))


def row_of_all(cold, hot):
    row = jnp.concatenate([cold.reshape(-1), hot])
    return jnp.pad(row, (0, -row.shape[0] % 128))[None, :]


def kernel(n_x, n_z, cold, listed, confidence, ratings, rated, owners, locals_, items, out,
           table, staged, message, msg_z, passed, msg_x, ids, ids_z, ids_x, ids_s, one, two, one_x_half, one_x, one_z_half, one_z,
           two_z_half, two_z, two_x,
           y_send, y_recv, c_send, c_recv, l_sem, a_send, a_recv, b_send, b_recv,
           one_x_sem, one_z_sem, two_z_sem, two_x_sem):
    dp = lax.axis_index("dp")
    y = lax.axis_index("rep")
    core = dp % 2
    z = (dp // 2) % n_z
    x = dp // (2 * n_z)
    n_y = 4

    def at(x_to, z_to):
        return ((x_to * n_z + z_to) * 2 + core, y)

    up, down, far = (y + 1) % n_y, (y + n_y - 1) % n_y, (y + 2) % n_y
    up_id, down_id, mate_id = (dp, up), (dp, down), (x * n_z * 2 + z * 2 + 1 - core, y)

    def remote(src, dst, send, recv, to):
        return pltpu.make_async_remote_copy(
            src_ref=src, dst_ref=dst, send_sem=send, recv_sem=recv, device_id=to, device_id_type=MESH)

    def each(count, body):
        for k in range(1, count):
            body(k)

    def others(ref, lead=()):
        index = lead + (pl.ds(0, ref.shape[len(lead)] - 1),)
        return ref.at[index]

    def waiter(ref, send, recv):
        return remote(ref, ref, send, recv, mate_id)

    barrier = pltpu.get_barrier_semaphore()
    for k in sorted(range(1, n_z), key=lambda k: -min(k, n_z - k)):
        pl.semaphore_signal(barrier, inc=1, device_id=at(x, (z + k) % n_z), device_id_type=MESH)
    each(n_x, lambda k: pl.semaphore_signal(
        barrier, inc=1, device_id=at((x + k) % n_x, z), device_id_type=MESH))
    for to in (up_id, down_id, mate_id):
        pl.semaphore_signal(barrier, inc=1, device_id=to, device_id_type=MESH)

    pairs = n_x * n_z
    width = owners.shape[1]
    owner_row = owners[...]
    owner_col = jnp.broadcast_to(owner_row, (8, width)).T[:, :1]
    before = lax.broadcasted_iota(i32, (width, width), 0) < lax.broadcasted_iota(i32, (width, width), 1)
    slot = jnp.sum(jnp.where((owner_col == owner_row) & before, 1, 0), axis=0, keepdims=True)
    number = lax.broadcasted_iota(i32, (1, width), 1)
    key = jnp.where(number < cold, owner_row * CAP + slot, jnp.where(number < listed, owner_row + 2 * pairs, -1))

    def wanted(pair, s):
        return 4 * pair + s if s < 4 else 4 * pairs + 2 * pair + s - 4

    entry = lax.broadcasted_iota(i32, (pairs, 1), 0)
    pair_of = (entry % n_x) * n_z + entry // n_x
    match = jnp.concatenate([key == wanted(pair_of, s) for s in range(6)], axis=0)
    rating_pick = jnp.where(match, 1.0, 0.0).astype(bf16)
    picked = []
    for u in range(2):
        weight_pick = jnp.where(match, rated[u:u + 1, :].astype(f32), 0.0).astype(bf16)
        picked.append(jnp.dot(weight_pick, confidence[u], preferred_element_type=f32))
    for u in range(2):
        picked.append(jnp.dot(rating_pick, ratings[u], preferred_element_type=f32))
    for n, lot in enumerate(picked):
        for j in range(3):
            both = [lot[(2 * j + i) * pairs:(2 * j + i + 1) * pairs] for i in range(2)]
            staged[pl.ds(3 * n + j, pairs, stride=12), :] = jnp.concatenate(both, axis=1)
    message[...] = staged[...].astype(bf16).reshape(message.shape)
    to_z_entry = lax.broadcasted_iota(i32, (n_z, 1), 0)
    lane = lax.broadcasted_iota(i32, (n_z, 128), 1)
    id_rows = jnp.zeros((n_z, 128), i32)
    for x_to in range(n_x):
        for s in range(6):
            hit = jnp.where(key == wanted(x_to * n_z + to_z_entry, s), locals_[...], 0)
            id_rows = id_rows + jnp.where(lane == 8 * x_to + s, jnp.sum(hit, axis=1, keepdims=True), 0)
    for z_to in range(n_z):
        ids[z_to] = id_rows[z_to:z_to + 1]

    pl.semaphore_wait(barrier, 3 + n_z - 1 + n_x - 1)

    held = items.shape[0]
    half = held // 2

    def rows(of_core, of_y, h):
        return table.at[of_core, pl.ds(of_y * held + h * half, half)]

    def own(h):
        return items.at[pl.ds(h * half, half)]

    def up_copy(k):
        if k < 2:
            return remote(own(k), rows(core, y, k), y_send.at[k], y_recv.at[k], up_id)
        return remote(rows(core, down, 0), rows(core, down, 0), y_send.at[2], y_recv.at[2], up_id)

    def down_copy(k):
        if k < 2:
            return remote(own(1 - k), rows(core, y, 1 - k), y_send.at[3 + k], y_recv.at[3 + k], down_id)
        return remote(rows(core, up, 1), rows(core, up, 1), y_send.at[5], y_recv.at[5], down_id)

    def from_down(k):
        ref = rows(core, down, k) if k < 2 else rows(core, far, 0)
        return remote(ref, ref, y_send.at[k], y_recv.at[k], up_id)

    def from_up(k):
        ref = rows(core, up, 1 - k) if k < 2 else rows(core, far, 1)
        return remote(ref, ref, y_send.at[3 + k], y_recv.at[3 + k], down_id)

    def mate_copy(n, src, of_y, h):
        return remote(src, rows(core, of_y, h), c_send.at[n], c_recv.at[n], mate_id)

    def from_mate(n, of_y, h):
        ref = rows(1 - core, of_y, h)
        return remote(ref, ref, c_send.at[n], c_recv.at[n], mate_id)

    for k in range(2):
        up_copy(k).start()
        down_copy(k).start()
    keep = pltpu.make_async_copy(items, table.at[core, pl.ds(y * held, held)], l_sem.at[0])
    keep.start()

    def place_of(k):
        return 0 if 2 * k == n_z else (n_z - 2 * k if 2 * k < n_z else 2 * k - n_z - 1)

    outer = n_z // 2 - 1
    spans = (pl.ds(0, outer), pl.ds(outer, n_z - outer))
    counts = (outer, n_z - outer - 1)

    def start_z(k):
        to = (z + k) % n_z
        lot = 0 if place_of(k) < outer else 1
        remote(message.at[to], msg_z.at[place_of(k)], a_send.at[0, lot], a_recv.at[0, lot], at(x, to)).start()
        remote(ids.at[to], ids_z.at[place_of(k)], a_send.at[1, lot], a_recv.at[1, lot], at(x, to)).start()

    def start_x(k, lot):
        to = (x + k) % n_x
        remote(passed.at[to, spans[lot]], msg_x.at[x, spans[lot]], b_send.at[0, lot], b_recv.at[0, lot], at(to, z)).start()
        remote(ids_z.at[spans[lot]], ids_x.at[x, spans[lot]], b_send.at[1, lot], b_recv.at[1, lot], at(to, z)).start()

    z_done, x_done = [], []
    for lot in range(2):
        some = pl.ds(0, counts[lot])
        z_done.append([waiter(msg_z.at[some], a_send.at[0, lot], a_recv.at[0, lot]),
                       waiter(ids_z.at[some], a_send.at[1, lot], a_recv.at[1, lot])])
        some = pl.ds(0, n_x - 1)
        x_done.append([waiter(msg_x.at[some, spans[lot]], b_send.at[0, lot], b_recv.at[0, lot]),
                       waiter(ids_x.at[some, spans[lot]], b_send.at[1, lot], b_recv.at[1, lot])])

    def pass_on(lot):
        for copy in z_done[lot]:
            copy.wait_recv()

        def part(n, carry):
            text = msg_z[n].astype(f32)
            for x_to in range(n_x):
                rows_to = jnp.concatenate([text[12 * x_to:12 * x_to + 12], jnp.zeros((4, 128), f32)], axis=0)
                passed[x_to, n] = rows_to.astype(bf16)
            return carry

        lax.fori_loop(spans[lot].start, spans[lot].start + spans[lot].size, part, 0)
        each(n_x, lambda k: start_x(k, lot))
        msg_x[x, spans[lot]] = passed[x, spans[lot]]
        ids_x[x, spans[lot]] = ids_z[spans[lot]]

    for k in sorted(range(1, n_z), key=place_of):
        start_z(k)
    for h in range(2):
        mate_copy(h, own(h), y, h).start()
    msg_z[n_z - 1] = message[z]
    ids_z[n_z - 1] = ids[z]

    from_down(0).wait_recv()
    up_copy(2).start()
    from_up(0).wait_recv()
    down_copy(2).start()
    mate_copy(2, rows(core, down, 0), down, 0).start()
    mate_copy(3, rows(core, up, 1), up, 1).start()

    pass_on(0)
    pass_on(1)

    from_down(1).wait_recv()
    mate_copy(4, rows(core, down, 1), down, 1).start()
    from_up(1).wait_recv()
    mate_copy(5, rows(core, up, 0), up, 0).start()

    for copy in x_done[0] + x_done[1]:
        copy.wait_recv()
    to_smem = pltpu.make_async_copy(ids_x, ids_s, l_sem.at[1])
    to_smem.start()

    from_down(2).wait_recv()
    mate_copy(6, rows(core, far, 0), far, 0).start()
    from_up(2).wait_recv()
    mate_copy(7, rows(core, far, 1), far, 1).start()

    for copy in z_done[0] + z_done[1] + x_done[0] + x_done[1]:
        copy.wait_send()
    for k in range(3):
        up_copy(k).wait_send()
        down_copy(k).wait_send()
    halves = [(y, 0), (y, 1), (down, 0), (up, 1), (down, 1), (up, 0), (far, 0), (far, 1)]
    for n, (of_y, h) in enumerate(halves):
        mate_copy(n, rows(core, of_y, h), of_y, h).wait_send()
    for n, (of_y, h) in enumerate(halves):
        from_mate(n, of_y, h).wait_recv()
    keep.wait()
    to_smem.wait()

    row_of = lax.broadcasted_iota(i32, (16, 128), 0)
    masks = [((row_of == 6 + j) | (row_of == 9 + j)).astype(f32) for j in range(3)]
    lane_block = lax.broadcasted_iota(i32, (8, 128), 1) // 8
    window = [(lane_block >= i) & (lane_block < i + 8) for i in range(8)]

    def build(place, carry):
        for p in range(n_x):
            build_one(p, place)
        return carry

    def build_one(p, place):
        xt = (x + (2, 1, 3, 0)[p]) % n_x
        found = [table[(0, 0, 1, 1, 0, 1)[s], ids_s[xt, place, 0, 8 * x + s]] for s in range(6)]
        chosen = jnp.concatenate(found, axis=0).T
        text = msg_x[xt, place].astype(f32)
        scaled = []
        for u in range(2):
            weight = jnp.concatenate(
                [jnp.broadcast_to(text[3 * u + j:3 * u + j + 1], (128, 128)) for j in range(3)], axis=1)
            scaled.append(chosen * weight.astype(bf16))
        scaled = jnp.concatenate(scaled, axis=0)
        rating = jnp.concatenate([(text * masks[j]).astype(bf16) for j in range(3)], axis=1)
        left = jnp.concatenate([chosen, rating], axis=0)
        both = lax.dot_general(left, scaled, (((1,), (1,)), ((), ())), preferred_element_type=f32)

        def group(u, i):
            return both[8 * i:8 * i + 8, 128 * u:128 * u + 128]

        main = [[jnp.where(window[i], group(u, i), group(u, i + 8)) for i in range(8)] for u in range(2)]
        shared = group(0, 0)
        for i in range(8):
            shared = jnp.where(lane_block == i + 8, group(0, i), shared)
            shared = jnp.where(lane_block == i, group(1, i + 8), shared)
        right = [
            jnp.sum(both[134 + 3 * u:137 + 3 * u, 128 * u:128 * u + 128], axis=0, keepdims=True)
            for u in range(2)
        ]
        packed = main[0] + main[1] + [shared, jnp.concatenate(right + [jnp.zeros((6, 128), f32)], axis=0)]
        one[p, place] = jnp.concatenate(packed[:one.shape[2] // 8], axis=0)
        two[p, place] = jnp.concatenate(packed[one.shape[2] // 8:], axis=0)

    last_x, last_z = n_x - 1, n_z - 1
    to_x = (at((x + 1) % n_x, z), at((x + n_x - 1) % n_x, z))
    to_z = (at(x, (z + 1) % n_z), at(x, (z + n_z - 1) % n_z))
    x_cuts = [cut for cut in X_CUTS if cut < n_z] + [n_z]
    x_lots = [pl.ds(cut, after - cut) for cut, after in zip(x_cuts, x_cuts[1:])]
    x_lot_of = [sum(cut <= n for cut in x_cuts) - 1 for n in range(n_z)]
    wide = n_x // LOTS_Z
    one_rows, two_rows = one.shape[2] // 2, two.shape[2] // 2
    steps_x, steps_z = n_x // 2, n_z // 2

    def place(way, step, steps):
        if step == steps:
            return 2 * steps - 1
        return 0 if step == 0 else 2 * step - 1 + way

    def one_x_copy(way, step, j):
        lots = x_lots[j]
        sems = one_x_sem.at[0, way, step, j], one_x_sem.at[1, way, step, j]
        if step == 0:
            return remote(one.at[0, lots, pl.ds(one_rows * way, one_rows)], one_x_half.at[way, lots], *sems, to_x[way])
        return remote(one.at[place(way, step, steps_x), lots], one_x.at[way, step - 1, lots], *sems, to_x[way])

    def one_z_copy(way, step):
        sems = one_z_sem.at[0, way, step], one_z_sem.at[1, way, step]
        if step == 0:
            return remote(one.at[last_x, 0, pl.ds(one_rows * way, one_rows)], one_z_half.at[way], *sems, to_z[way])
        return remote(one.at[last_x, place(way, step, steps_z)], one_z.at[way, step - 1], *sems, to_z[way])

    def two_z_copy(way, step, p):
        sems = two_z_sem.at[0, way, step, p], two_z_sem.at[1, way, step, p]
        lot = pl.ds(p * wide, wide)
        if step == 0:
            return remote(two.at[lot, 0, pl.ds(two_rows * way, two_rows)], two_z_half.at[way, lot], *sems, to_z[way])
        return remote(two.at[lot, place(way, step, steps_z)], two_z.at[way, step - 1, lot], *sems, to_z[way])

    def two_x_copy(p):
        ahead = (2, 1, 3)[p]
        sems = two_x_sem.at[0, p], two_x_sem.at[1, p]
        return remote(two.at[p, last_z], two_x.at[p], *sems, at((x + ahead) % n_x, z))

    delay, event_us, build_us = 2.5, 0.15, 0.5
    clock = {"now": 0.0, "x": 0.0, "z": 0.0}
    built, serial, pending, done_x, done_z = [0], [0], [], [], []

    def sent(axis, rows_sent, event, args):
        clock[axis] = max(clock[axis], clock["now"]) + rows_sent * 2 * 512 / 1e5
        serial[0] += 1
        pending.append((clock[axis] + delay, serial[0], event, args))

    def start_one_x(step, j):
        for way in range(2):
            one_x_copy(way, step, j).start()
        sent("x", x_lots[j].size * one_rows * (2 if step else 1), one_x_event, (step, j))

    def start_one_z(step):
        for way in range(2):
            one_z_copy(way, step).start()
        sent("z", one_rows * (2 if step else 1), one_z_event, (step,))

    def start_two_z(step, p):
        for way in range(2):
            two_z_copy(way, step, p).start()
        sent("z", wide * two_rows * (2 if step else 1), two_z_event, (step, p))

    def start_two_x():
        for p in range(last_x):
            two_x_copy(p).start()
        sent("x", 4 * two_rows, two_x_event, ())

    def ready_one_z():
        step = len(done_z)
        needed = x_lot_of[max(place(way, step, steps_z) for way in range(2))]
        if step < steps_z and set(range(needed + 1)) <= set(done_x) and ("one", step) not in begun:
            begun.add(("one", step))
            start_one_z(step)

    begun = set()

    def one_x_event(step, j):
        for way in range(2):
            one_x_copy(way, step, j).wait()
            lots = x_lots[j]
            at_place = place(way, step + 1, steps_x)
            if step == 0:
                one[at_place, lots, pl.ds(one_rows * way, one_rows)] += one_x_half[way, lots]
            else:
                one[at_place, lots] += one_x[way, step - 1, lots]
        if step + 1 < steps_x:
            start_one_x(step + 1, j)
            if j + 2 < len(x_lots):
                first_one_x(j + 2)
        else:
            done_x.append(j)
            ready_one_z()

    def one_z_event(step):
        for way in range(2):
            one_z_copy(way, step).wait()
            at_place = place(way, step + 1, steps_z)
            if step == 0:
                one[last_x, at_place, pl.ds(one_rows * way, one_rows)] += one_z_half[way]
            else:
                one[last_x, at_place] += one_z[way, step - 1]
        done_z.append(step)
        ready_one_z()

    def two_z_event(step, p):
        lot = pl.ds(p * wide, wide)
        for way in range(2):
            two_z_copy(way, step, p).wait()
            at_place = place(way, step + 1, steps_z)
            while at_place >= built[0]:
                build_some()
            if step == 0:
                two[lot, at_place, pl.ds(two_rows * way, two_rows)] += two_z_half[way, lot]
            else:
                two[lot, at_place] += two_z[way, step - 1, lot]
        if step + 1 < steps_z:
            start_two_z(step + 1, p)
        elif p == n_x // wide - 1:
            start_two_x()

    def two_x_event():
        for p in range(last_x):
            two_x_copy(p).wait()
        two[last_x, last_z] += two_x[0] + two_x[1] + two_x[2]

    def build_some():
        first = built[0]
        size = 1 if first == 0 else n_z // 4 - first % (n_z // 4)
        lax.fori_loop(first, first + size, build, 0)
        built[0] += size
        clock["now"] += build_us * size
        if first == 0:
            for p in range(n_x // wide):
                start_two_z(0, p)
        for j in range(min(2, len(x_lots))):
            if first < x_cuts[j + 1] <= built[0]:
                start_one_x(0, j)

    def first_one_x(j):
        while built[0] < x_cuts[j + 1]:
            build_some()
        start_one_x(0, j)

    while pending or built[0] < n_z:
        pending.sort()
        if built[0] < n_z and not (pending and pending[0][0] <= clock["now"]):
            build_some()
            continue
        arrival, _, event, args = pending.pop(0)
        clock["now"] = max(clock["now"], arrival) + event_us
        event(*args)

    row_block = lax.broadcasted_iota(i32, (128, 128), 0) // 8
    own_block = row_block == lax.broadcasted_iota(i32, (128, 128), 1) // 8
    lot = jnp.concatenate([one[last_x, last_z], two[last_x, last_z]], axis=0)
    grams = []
    for u in range(2):
        main = lot[64 * u:64 * u + 64]
        upper = [jnp.where(window[i], main[8 * i:8 * i + 8], 0.0) for i in range(8)]
        lower = [jnp.where(window[i], 0.0, main[8 * i:8 * i + 8]) for i in range(8)]
        for i in range(8):
            if u == 0:
                upper[i] = jnp.where(lane_block == i + 8, lot[128:136], upper[i])
            else:
                lower[i] = jnp.where(lane_block == i, lot[128:136], lower[i])
        kept = jnp.concatenate(upper + lower, axis=0)
        grams.append(kept + jnp.where(own_block, 0.0, kept).T)
    right = lot[136:138]

    def iterate(n, state):
        answer, residual, direction, norm = state
        turned = jnp.concatenate([direction, jnp.zeros((6, 128), f32)], axis=0).T
        image = jnp.concatenate(
            [jnp.sum(grams[u] * turned[:, u:u + 1], axis=0, keepdims=True) for u in range(2)], axis=0)
        image = image + 0.1 * direction
        step = norm / jnp.sum(direction * image, axis=-1, keepdims=True)
        answer = answer + step * direction
        residual = residual - step * image
        after = jnp.sum(residual * residual, axis=-1, keepdims=True)
        direction = residual + (after / norm) * direction
        return answer, residual, direction, after

    state = (jnp.zeros_like(right), right, right, jnp.sum(right * right, axis=-1, keepdims=True))
    for n in range(ITERS):
        state = iterate(n, state)
    out[...] = state[0]


def body(n_x, n_z, ratings, confidence, rated, item_factors, cold_owner, cold_local, hot_group, hot_local):
    users = confidence.shape[0]
    cold, listed = cold_owner.size, rated.shape[1]
    rows, width = item_factors.shape
    vmem = pl.BlockSpec(memory_space=pltpu.VMEM)
    dma = pltpu.SemaphoreType.DMA
    return pl.pallas_call(
        functools.partial(kernel, n_x, n_z, cold, listed),
        out_shape=jax.ShapeDtypeStruct((users, width), f32),
        in_specs=[vmem] * 5 + [pl.BlockSpec(memory_space=pl.ANY)],
        out_specs=vmem,
        scratch_shapes=[
            pltpu.VMEM((2, 4 * rows // BLK, BLK, width), bf16),
            pltpu.VMEM((n_z * n_x * 12, width), f32),
            pltpu.VMEM((n_z, n_x * 12, width), bf16),
            pltpu.VMEM((n_z, n_x * 12, width), bf16),
            pltpu.VMEM((n_x, n_z, 16, width), bf16),
            pltpu.VMEM((n_x, n_z, 16, width), bf16),
            pltpu.VMEM((n_z, 1, 128), i32),
            pltpu.VMEM((n_z, 1, 128), i32),
            pltpu.VMEM((n_x, n_z, 1, 128), i32),
            pltpu.SMEM((n_x, n_z, 1, 128), i32),
            pltpu.VMEM((n_x, n_z, ONE_ROWS, width), f32),
            pltpu.VMEM((n_x, n_z, TWO_ROWS, width), f32),
            pltpu.VMEM((2, n_z, ONE_ROWS // 2, width), f32),
            pltpu.VMEM((2, n_x // 2 - 1, n_z, ONE_ROWS, width), f32),
            pltpu.VMEM((2, ONE_ROWS // 2, width), f32),
            pltpu.VMEM((2, n_z // 2 - 1, ONE_ROWS, width), f32),
            pltpu.VMEM((2, n_x, TWO_ROWS // 2, width), f32),
            pltpu.VMEM((2, n_z // 2 - 1, n_x, TWO_ROWS, width), f32),
            pltpu.VMEM((n_x - 1, TWO_ROWS, width), f32),
            dma((6,)), dma((6,)), dma((8,)), dma((8,)), dma((2,)),
            dma((2, 2)), dma((2, 2)), dma((2, 2)), dma((2, 2)),
            dma((2, 2, n_x // 2, len(X_CUTS))), dma((2, 2, n_z // 2)), dma((2, 2, n_z // 2, LOTS_Z)), dma((2, n_x - 1)),
        ],
        compiler_params=pltpu.CompilerParams(
            collective_id=0, has_side_effects=True, vmem_limit_bytes=40 * 1024 * 1024),
    )(
        blocks_of(confidence), blocks_of(ratings),
        jnp.pad(rated, ((0, 0), (0, -listed % 128))),
        row_of_all(cold_owner, hot_group + 2 * n_x * n_z), row_of_all(cold_local, hot_local),
        item_factors.reshape(-1, BLK, width))


def solution(mesh):
    n_dp = mesh.shape["dp"]
    n_x = N_X
    n_z = n_dp // (2 * n_x)
    in_specs = (
        P(("dp", "rep"), None),
        P(("dp", "rep"), None),
        P(("dp", "rep"), None),
        P(("dp", "rep"), None),
        P("dp", "rep", None, None),
        P("dp", "rep", None),
        P(),
        P(),
    )
    return jax.shard_map(
        functools.partial(body, n_x, n_z), mesh=mesh, in_specs=in_specs,
        out_specs=P(("dp", "rep"), None), check_vma=False)
```

```python
import functools

import jax
import jax.numpy as jnp
from jax import lax
from jax.experimental import pallas as pl
from jax.experimental.pallas import tpu as pltpu
from jax.sharding import PartitionSpec as P

BLK = 64
CAP = 2
ITERS = 3
N_X = 4
PACKED_ROWS = 144
ONE_ROWS = 80
TWO_ROWS = PACKED_ROWS - ONE_ROWS
X_CUTS = (0, 1, 3, 5, 7, 11)
LOTS_Z = 4
MESH = pl.DeviceIdType.MESH
bf16, f32, i32 = jnp.bfloat16, jnp.float32, jnp.int32


def kernel(n_x, n_z, confidence_in, ratings_in, rated_in, owners_in, locals_in, hot_group_in, hot_local_in, items, out,
           confidence, ratings, rated, owners, locals_, hot_group, hot_local, pairs_of, lined, in_sem,
           table, staged, message, msg_z, passed, msg_x, ids, ids_z, ids_x, ids_s, one, two, one_x_half, one_x, one_z_half, one_z,
           two_z_half, two_z, two_x,
           y_send, y_recv, c_send, c_recv, l_sem, a_send, a_recv, b_send, b_recv,
           one_x_sem, one_z_sem, two_z_sem, two_x_sem):
    dp = lax.axis_index("dp")
    y = lax.axis_index("rep")
    core = dp % 2
    z = (dp // 2) % n_z
    x = dp // (2 * n_z)
    n_y = 4

    def at(x_to, z_to):
        return ((x_to * n_z + z_to) * 2 + core, y)

    up, down, far = (y + 1) % n_y, (y + n_y - 1) % n_y, (y + 2) % n_y
    up_id, down_id, mate_id = (dp, up), (dp, down), (x * n_z * 2 + z * 2 + 1 - core, y)

    def remote(src, dst, send, recv, to):
        return pltpu.make_async_remote_copy(
            src_ref=src, dst_ref=dst, send_sem=send, recv_sem=recv, device_id=to, device_id_type=MESH)

    def each(count, body):
        for k in range(1, count):
            body(k)

    def others(ref, lead=()):
        index = lead + (pl.ds(0, ref.shape[len(lead)] - 1),)
        return ref.at[index]

    def waiter(ref, send, recv):
        return remote(ref, ref, send, recv, mate_id)

    barrier = pltpu.get_barrier_semaphore()
    for k in sorted(range(1, n_z), key=lambda k: -min(k, n_z - k)):
        pl.semaphore_signal(barrier, inc=1, device_id=at(x, (z + k) % n_z), device_id_type=MESH)
    each(n_x, lambda k: pl.semaphore_signal(
        barrier, inc=1, device_id=at((x + k) % n_x, z), device_id_type=MESH))
    for to in (up_id, down_id, mate_id):
        pl.semaphore_signal(barrier, inc=1, device_id=to, device_id_type=MESH)

    given = (confidence_in, ratings_in, rated_in, owners_in, locals_in, hot_group_in, hot_local_in)
    held_in = (confidence, ratings, rated, owners, locals_, hot_group, hot_local)
    inputs = [pltpu.make_async_copy(a, b, in_sem.at[n]) for n, (a, b) in enumerate(zip(given, held_in))]
    for copy in inputs:
        copy.start()

    pairs = n_x * n_z
    for copy in inputs:
        copy.wait()
    cold, hot = owners.shape[1], hot_group.shape[1]
    listed = cold + hot
    width = listed + -listed % 128

    def row_of(cold_part, hot_part):
        return jnp.concatenate([cold_part, hot_part, jnp.zeros((1, width - listed), i32)], axis=1)

    owner_row = row_of(owners[...], hot_group[...] + 2 * pairs)
    local_row = row_of(locals_[...], hot_local[...])

    def two_blocks(k, carry):
        lanes = pl.ds(pl.multiple_of(128 * k, 128), 128)
        for n, given in enumerate((confidence, ratings)):
            lot = given[:, lanes].astype(f32)
            for u in range(2):
                pairs_of[2 * n + u, pl.ds(k, 1), :] = lot[u:u + 1]
        return carry

    lax.fori_loop(0, listed // 2, two_blocks, 0, unroll=4)
    for n in range(4):
        lined[n, pl.ds(listed, width - listed), :] = jnp.zeros((width - listed, 128), f32)
        lot = pairs_of[n]
        lined[n, pl.ds(0, listed // 2, stride=2), :] = lot
        lined[n, pl.ds(1, listed // 2, stride=2), :] = jnp.concatenate([lot[:, BLK:], lot[:, :BLK]], axis=1)
    owner_col = jnp.broadcast_to(owner_row, (8, width)).T[:, :1]
    before = lax.broadcasted_iota(i32, (width, width), 0) < lax.broadcasted_iota(i32, (width, width), 1)
    slot = jnp.sum(jnp.where((owner_col == owner_row) & before, 1, 0), axis=0, keepdims=True)
    number = lax.broadcasted_iota(i32, (1, width), 1)
    key = jnp.where(number < cold, owner_row * CAP + slot, jnp.where(number < listed, owner_row + 2 * pairs, -1))

    def wanted(pair, s):
        return 4 * pair + s if s < 4 else 4 * pairs + 2 * pair + s - 4

    entry = lax.broadcasted_iota(i32, (pairs, 1), 0)
    pair_of = (entry % n_x) * n_z + entry // n_x
    match = jnp.concatenate([key == wanted(pair_of, s) for s in range(6)], axis=0)
    rating_pick = jnp.where(match, 1.0, 0.0).astype(bf16)
    picked = []
    for u in range(2):
        rated_row = jnp.concatenate([rated[u:u + 1, :], jnp.zeros((1, width - listed), i32)], axis=1)
        weight_pick = jnp.where(match, rated_row.astype(f32), 0.0).astype(bf16)
        picked.append(jnp.dot(weight_pick, lined[u].astype(bf16), preferred_element_type=f32))
    for u in range(2):
        picked.append(jnp.dot(rating_pick, lined[2 + u].astype(bf16), preferred_element_type=f32))
    for n, lot in enumerate(picked):
        for j in range(3):
            both = [lot[(2 * j + i) * pairs:(2 * j + i + 1) * pairs, :BLK] for i in range(2)]
            staged[pl.ds(3 * n + j, pairs, stride=12), :] = jnp.concatenate(both, axis=1)
    message[...] = staged[...].astype(bf16).reshape(message.shape)
    to_z_entry = lax.broadcasted_iota(i32, (n_z, 1), 0)
    lane = lax.broadcasted_iota(i32, (n_z, 128), 1)
    id_rows = jnp.zeros((n_z, 128), i32)
    for x_to in range(n_x):
        for s in range(6):
            hit = jnp.where(key == wanted(x_to * n_z + to_z_entry, s), local_row, 0)
            id_rows = id_rows + jnp.where(lane == 8 * x_to + s, jnp.sum(hit, axis=1, keepdims=True), 0)
    for z_to in range(n_z):
        ids[z_to] = id_rows[z_to:z_to + 1]

    pl.semaphore_wait(barrier, 3 + n_z - 1 + n_x - 1)

    held = items.shape[0]
    half = held // 2

    def rows(of_core, of_y, h):
        return table.at[of_core, pl.ds(of_y * held + h * half, half)]

    fourth = half // 2

    def fourths(of_core, of_y, q):
        return table.at[of_core, pl.ds(of_y * held + q * fourth, fourth)]

    def own(h):
        return items.at[pl.ds(h * half, half)]

    def up_copy(k):
        if k < 2:
            return remote(own(k), rows(core, y, k), y_send.at[k], y_recv.at[k], up_id)
        return remote(fourths(core, down, k - 2), fourths(core, down, k - 2), y_send.at[k], y_recv.at[k], up_id)

    def down_copy(k):
        if k < 2:
            return remote(own(1 - k), rows(core, y, 1 - k), y_send.at[4 + k], y_recv.at[4 + k], down_id)
        return remote(fourths(core, up, k), fourths(core, up, k), y_send.at[4 + k], y_recv.at[4 + k], down_id)

    def from_down(k):
        ref = rows(core, down, k) if k < 2 else fourths(core, far, k - 2)
        return remote(ref, ref, y_send.at[k], y_recv.at[k], up_id)

    def from_up(k):
        ref = rows(core, up, 1 - k) if k < 2 else fourths(core, far, k)
        return remote(ref, ref, y_send.at[4 + k], y_recv.at[4 + k], down_id)

    def lot_of(n, of_core, of_y, h):
        return rows(of_core, of_y, h) if n < 6 else fourths(of_core, of_y, h)

    def mate_copy(n, src, of_y, h):
        return remote(src, lot_of(n, core, of_y, h), c_send.at[n], c_recv.at[n], mate_id)

    def from_mate(n, of_y, h):
        ref = lot_of(n, 1 - core, of_y, h)
        return remote(ref, ref, c_send.at[n], c_recv.at[n], mate_id)

    for k in range(2):
        up_copy(k).start()
        down_copy(k).start()
    keep = pltpu.make_async_copy(items, table.at[core, pl.ds(y * held, held)], l_sem.at[0])
    keep.start()

    def place_of(k):
        return 0 if 2 * k == n_z else (n_z - 2 * k if 2 * k < n_z else 2 * k - n_z - 1)

    outer = n_z // 2 - 1
    spans = (pl.ds(0, outer), pl.ds(outer, n_z - outer))
    counts = (outer, n_z - outer - 1)

    def start_z(k):
        to = (z + k) % n_z
        lot = 0 if place_of(k) < outer else 1
        remote(message.at[to], msg_z.at[place_of(k)], a_send.at[0, lot], a_recv.at[0, lot], at(x, to)).start()
        remote(ids.at[to], ids_z.at[place_of(k)], a_send.at[1, lot], a_recv.at[1, lot], at(x, to)).start()

    def start_x(k, lot):
        to = (x + k) % n_x
        remote(passed.at[to, spans[lot]], msg_x.at[x, spans[lot]], b_send.at[0, lot], b_recv.at[0, lot], at(to, z)).start()
        remote(ids_z.at[spans[lot]], ids_x.at[x, spans[lot]], b_send.at[1, lot], b_recv.at[1, lot], at(to, z)).start()

    z_done, x_done = [], []
    for lot in range(2):
        some = pl.ds(0, counts[lot])
        z_done.append([waiter(msg_z.at[some], a_send.at[0, lot], a_recv.at[0, lot]),
                       waiter(ids_z.at[some], a_send.at[1, lot], a_recv.at[1, lot])])
        some = pl.ds(0, n_x - 1)
        x_done.append([waiter(msg_x.at[some, spans[lot]], b_send.at[0, lot], b_recv.at[0, lot]),
                       waiter(ids_x.at[some, spans[lot]], b_send.at[1, lot], b_recv.at[1, lot])])

    def pass_on(lot):
        for copy in z_done[lot]:
            copy.wait_recv()

        def part(n, carry):
            text = msg_z[n].astype(f32)
            for x_to in range(n_x):
                rows_to = jnp.concatenate([text[12 * x_to:12 * x_to + 12], jnp.zeros((4, 128), f32)], axis=0)
                passed[x_to, n] = rows_to.astype(bf16)
            return carry

        lax.fori_loop(spans[lot].start, spans[lot].start + spans[lot].size, part, 0)
        each(n_x, lambda k: start_x(k, lot))
        msg_x[x, spans[lot]] = passed[x, spans[lot]]
        ids_x[x, spans[lot]] = ids_z[spans[lot]]

    for k in sorted(range(1, n_z), key=place_of):
        start_z(k)
    for h in range(2):
        mate_copy(h, own(h), y, h).start()
    msg_z[n_z - 1] = message[z]
    ids_z[n_z - 1] = ids[z]

    from_down(0).wait_recv()
    up_copy(2).start()
    up_copy(3).start()
    from_up(0).wait_recv()
    down_copy(2).start()
    down_copy(3).start()
    mate_copy(2, rows(core, down, 0), down, 0).start()
    mate_copy(3, rows(core, up, 1), up, 1).start()

    pass_on(0)
    pass_on(1)

    from_down(1).wait_recv()
    mate_copy(4, rows(core, down, 1), down, 1).start()
    from_up(1).wait_recv()
    mate_copy(5, rows(core, up, 0), up, 0).start()

    for copy in x_done[0] + x_done[1]:
        copy.wait_recv()
    to_smem = pltpu.make_async_copy(ids_x, ids_s, l_sem.at[1])
    to_smem.start()

    for k in range(2):
        from_down(2 + k).wait_recv()
        mate_copy(6 + 2 * k, fourths(core, far, k), far, k).start()
        from_up(2 + k).wait_recv()
        mate_copy(7 + 2 * k, fourths(core, far, 2 + k), far, 2 + k).start()

    for copy in z_done[0] + z_done[1] + x_done[0] + x_done[1]:
        copy.wait_send()
    for k in range(4):
        up_copy(k).wait_send()
        down_copy(k).wait_send()
    halves = [(y, 0), (y, 1), (down, 0), (up, 1), (down, 1), (up, 0), (far, 0), (far, 2), (far, 1), (far, 3)]
    for n, (of_y, h) in enumerate(halves):
        mate_copy(n, lot_of(n, core, of_y, h), of_y, h).wait_send()
    for n, (of_y, h) in enumerate(halves):
        from_mate(n, of_y, h).wait_recv()
    keep.wait()
    to_smem.wait()

    row_of = lax.broadcasted_iota(i32, (16, 128), 0)
    masks = [((row_of == 6 + j) | (row_of == 9 + j)).astype(f32) for j in range(3)]
    lane_block = lax.broadcasted_iota(i32, (8, 128), 1) // 8
    window = [(lane_block >= i) & (lane_block < i + 8) for i in range(8)]

    def build(place, carry):
        for p in range(n_x):
            build_one(p, place)
        return carry

    def build_one(p, place):
        xt = (x + (2, 1, 3, 0)[p]) % n_x
        found = [table[(0, 0, 1, 1, 0, 1)[s], ids_s[xt, place, 0, 8 * x + s]] for s in range(6)]
        chosen = jnp.concatenate(found, axis=0).T
        text = msg_x[xt, place].astype(f32)
        scaled = []
        for u in range(2):
            weight = jnp.concatenate(
                [jnp.broadcast_to(text[3 * u + j:3 * u + j + 1], (128, 128)) for j in range(3)], axis=1)
            scaled.append(chosen * weight.astype(bf16))
        scaled = jnp.concatenate(scaled, axis=0)
        rating = jnp.concatenate([(text * masks[j]).astype(bf16) for j in range(3)], axis=1)
        left = jnp.concatenate([chosen, rating], axis=0)
        both = lax.dot_general(left, scaled, (((1,), (1,)), ((), ())), preferred_element_type=f32)

        def group(u, i):
            return both[8 * i:8 * i + 8, 128 * u:128 * u + 128]

        main = [[jnp.where(window[i], group(u, i), group(u, i + 8)) for i in range(8)] for u in range(2)]
        shared = group(0, 0)
        for i in range(8):
            shared = jnp.where(lane_block == i + 8, group(0, i), shared)
            shared = jnp.where(lane_block == i, group(1, i + 8), shared)
        right = [
            jnp.sum(both[134 + 3 * u:137 + 3 * u, 128 * u:128 * u + 128], axis=0, keepdims=True)
            for u in range(2)
        ]
        packed = main[0] + main[1] + [shared, jnp.concatenate(right + [jnp.zeros((6, 128), f32)], axis=0)]
        one[p, place] = jnp.concatenate(packed[:one.shape[2] // 8], axis=0)
        two[p, place] = jnp.concatenate(packed[one.shape[2] // 8:], axis=0)

    last_x, last_z = n_x - 1, n_z - 1
    to_x = (at((x + 1) % n_x, z), at((x + n_x - 1) % n_x, z))
    to_z = (at(x, (z + 1) % n_z), at(x, (z + n_z - 1) % n_z))
    x_cuts = [cut for cut in X_CUTS if cut < n_z] + [n_z]
    x_lots = [pl.ds(cut, after - cut) for cut, after in zip(x_cuts, x_cuts[1:])]
    x_lot_of = [sum(cut <= n for cut in x_cuts) - 1 for n in range(n_z)]
    wide = n_x // LOTS_Z
    one_rows, two_rows = one.shape[2] // 2, two.shape[2] // 2
    steps_x, steps_z = n_x // 2, n_z // 2

    def place(way, step, steps):
        if step == steps:
            return 2 * steps - 1
        return 0 if step == 0 else 2 * step - 1 + way

    def one_x_copy(way, step, j):
        lots = x_lots[j]
        sems = one_x_sem.at[0, way, step, j], one_x_sem.at[1, way, step, j]
        if step == 0:
            return remote(one.at[0, lots, pl.ds(one_rows * way, one_rows)], one_x_half.at[way, lots], *sems, to_x[way])
        return remote(one.at[place(way, step, steps_x), lots], one_x.at[way, step - 1, lots], *sems, to_x[way])

    def one_z_copy(way, step):
        sems = one_z_sem.at[0, way, step], one_z_sem.at[1, way, step]
        if step == 0:
            return remote(one.at[last_x, 0, pl.ds(one_rows * way, one_rows)], one_z_half.at[way], *sems, to_z[way])
        return remote(one.at[last_x, place(way, step, steps_z)], one_z.at[way, step - 1], *sems, to_z[way])

    def two_z_copy(way, step, p):
        sems = two_z_sem.at[0, way, step, p], two_z_sem.at[1, way, step, p]
        lot = pl.ds(p * wide, wide)
        if step == 0:
            return remote(two.at[lot, 0, pl.ds(two_rows * way, two_rows)], two_z_half.at[way, lot], *sems, to_z[way])
        return remote(two.at[lot, place(way, step, steps_z)], two_z.at[way, step - 1, lot], *sems, to_z[way])

    def two_x_copy(p):
        ahead = (2, 1, 3)[p]
        sems = two_x_sem.at[0, p], two_x_sem.at[1, p]
        return remote(two.at[p, last_z], two_x.at[p], *sems, at((x + ahead) % n_x, z))

    delay, event_us, build_us = 2.5, 0.15, 0.5
    clock = {"now": 0.0, "x": 0.0, "z": 0.0}
    built, serial, pending, done_x, done_z = [0], [0], [], [], []

    def sent(axis, rows_sent, event, args):
        clock[axis] = max(clock[axis], clock["now"]) + rows_sent * 2 * 512 / 1e5
        serial[0] += 1
        pending.append((clock[axis] + delay, serial[0], event, args))

    def start_one_x(step, j):
        for way in range(2):
            one_x_copy(way, step, j).start()
        sent("x", x_lots[j].size * one_rows * (2 if step else 1), one_x_event, (step, j))

    def start_one_z(step):
        for way in range(2):
            one_z_copy(way, step).start()
        sent("z", one_rows * (2 if step else 1), one_z_event, (step,))

    def start_two_z(step, p):
        for way in range(2):
            two_z_copy(way, step, p).start()
        sent("z", wide * two_rows * (2 if step else 1), two_z_event, (step, p))

    def start_two_x():
        for p in range(last_x):
            two_x_copy(p).start()
        sent("x", 4 * two_rows, two_x_event, ())

    def ready_one_z():
        step = len(done_z)
        needed = x_lot_of[max(place(way, step, steps_z) for way in range(2))]
        if step < steps_z and set(range(needed + 1)) <= set(done_x) and ("one", step) not in begun:
            begun.add(("one", step))
            start_one_z(step)

    begun = set()

    def one_x_event(step, j):
        for way in range(2):
            one_x_copy(way, step, j).wait()
            lots = x_lots[j]
            at_place = place(way, step + 1, steps_x)
            if step == 0:
                one[at_place, lots, pl.ds(one_rows * way, one_rows)] += one_x_half[way, lots]
            else:
                one[at_place, lots] += one_x[way, step - 1, lots]
        if step + 1 < steps_x:
            start_one_x(step + 1, j)
            if j + 2 < len(x_lots):
                first_one_x(j + 2)
        else:
            done_x.append(j)
            ready_one_z()

    def one_z_event(step):
        for way in range(2):
            one_z_copy(way, step).wait()
            at_place = place(way, step + 1, steps_z)
            if step == 0:
                one[last_x, at_place, pl.ds(one_rows * way, one_rows)] += one_z_half[way]
            else:
                one[last_x, at_place] += one_z[way, step - 1]
        done_z.append(step)
        ready_one_z()

    def two_z_event(step, p):
        lot = pl.ds(p * wide, wide)
        for way in range(2):
            two_z_copy(way, step, p).wait()
            at_place = place(way, step + 1, steps_z)
            while at_place >= built[0]:
                build_some()
            if step == 0:
                two[lot, at_place, pl.ds(two_rows * way, two_rows)] += two_z_half[way, lot]
            else:
                two[lot, at_place] += two_z[way, step - 1, lot]
        if step + 1 < steps_z:
            start_two_z(step + 1, p)
        elif p == n_x // wide - 1:
            start_two_x()

    def two_x_event():
        for p in range(last_x):
            two_x_copy(p).wait()
        two[last_x, last_z] += two_x[0] + two_x[1] + two_x[2]

    def build_some():
        first = built[0]
        size = 1 if first == 0 else n_z // 4 - first % (n_z // 4)
        lax.fori_loop(first, first + size, build, 0)
        built[0] += size
        clock["now"] += build_us * size
        if first == 0:
            for p in range(n_x // wide):
                start_two_z(0, p)
        for j in range(min(2, len(x_lots))):
            if first < x_cuts[j + 1] <= built[0]:
                start_one_x(0, j)

    def first_one_x(j):
        while built[0] < x_cuts[j + 1]:
            build_some()
        start_one_x(0, j)

    while pending or built[0] < n_z:
        pending.sort()
        if built[0] < n_z and not (pending and pending[0][0] <= clock["now"]):
            build_some()
            continue
        arrival, _, event, args = pending.pop(0)
        clock["now"] = max(clock["now"], arrival) + event_us
        event(*args)

    row_block = lax.broadcasted_iota(i32, (128, 128), 0) // 8
    own_block = row_block == lax.broadcasted_iota(i32, (128, 128), 1) // 8
    lot = jnp.concatenate([one[last_x, last_z], two[last_x, last_z]], axis=0)
    grams = []
    for u in range(2):
        main = lot[64 * u:64 * u + 64]
        upper = [jnp.where(window[i], main[8 * i:8 * i + 8], 0.0) for i in range(8)]
        lower = [jnp.where(window[i], 0.0, main[8 * i:8 * i + 8]) for i in range(8)]
        for i in range(8):
            if u == 0:
                upper[i] = jnp.where(lane_block == i + 8, lot[128:136], upper[i])
            else:
                lower[i] = jnp.where(lane_block == i, lot[128:136], lower[i])
        kept = jnp.concatenate(upper + lower, axis=0)
        grams.append(kept + jnp.where(own_block, 0.0, kept).T)
    right = lot[136:138]

    def iterate(n, state):
        answer, residual, direction, norm = state
        turned = jnp.concatenate([direction, jnp.zeros((6, 128), f32)], axis=0).T
        image = jnp.concatenate(
            [jnp.sum(grams[u] * turned[:, u:u + 1], axis=0, keepdims=True) for u in range(2)], axis=0)
        image = image + 0.1 * direction
        step = norm / jnp.sum(direction * image, axis=-1, keepdims=True)
        answer = answer + step * direction
        residual = residual - step * image
        after = jnp.sum(residual * residual, axis=-1, keepdims=True)
        direction = residual + (after / norm) * direction
        return answer, residual, direction, after

    state = (jnp.zeros_like(right), right, right, jnp.sum(right * right, axis=-1, keepdims=True))
    for n in range(ITERS):
        state = iterate(n, state)
    out[...] = state[0]


def body(n_x, n_z, ratings, confidence, rated, item_factors, cold_owner, cold_local, hot_group, hot_local):
    users = confidence.shape[0]
    small = (confidence, ratings, rated, cold_owner.reshape(1, -1), cold_local.reshape(1, -1),
             hot_group.reshape(1, -1), hot_local.reshape(1, -1))
    listed = rated.shape[1]
    lines = listed + -listed % 128
    rows, width = item_factors.shape
    vmem = pl.BlockSpec(memory_space=pltpu.VMEM)
    dma = pltpu.SemaphoreType.DMA
    return pl.pallas_call(
        functools.partial(kernel, n_x, n_z),
        out_shape=jax.ShapeDtypeStruct((users, width), f32),
        in_specs=[pl.BlockSpec(memory_space=pl.ANY)] * 8,
        out_specs=vmem,
        scratch_shapes=[pltpu.VMEM(a.shape, a.dtype) for a in small] + [
            pltpu.VMEM((2 * users, listed // 2, width), f32),
            pltpu.VMEM((2 * users, lines, width), f32),
            dma((len(small),)),
            pltpu.VMEM((2, 4 * rows // BLK, BLK, width), bf16),
            pltpu.VMEM((n_z * n_x * 12, width), f32),
            pltpu.VMEM((n_z, n_x * 12, width), bf16),
            pltpu.VMEM((n_z, n_x * 12, width), bf16),
            pltpu.VMEM((n_x, n_z, 16, width), bf16),
            pltpu.VMEM((n_x, n_z, 16, width), bf16),
            pltpu.VMEM((n_z, 1, 128), i32),
            pltpu.VMEM((n_z, 1, 128), i32),
            pltpu.VMEM((n_x, n_z, 1, 128), i32),
            pltpu.SMEM((n_x, n_z, 1, 128), i32),
            pltpu.VMEM((n_x, n_z, ONE_ROWS, width), f32),
            pltpu.VMEM((n_x, n_z, TWO_ROWS, width), f32),
            pltpu.VMEM((2, n_z, ONE_ROWS // 2, width), f32),
            pltpu.VMEM((2, n_x // 2 - 1, n_z, ONE_ROWS, width), f32),
            pltpu.VMEM((2, ONE_ROWS // 2, width), f32),
            pltpu.VMEM((2, n_z // 2 - 1, ONE_ROWS, width), f32),
            pltpu.VMEM((2, n_x, TWO_ROWS // 2, width), f32),
            pltpu.VMEM((2, n_z // 2 - 1, n_x, TWO_ROWS, width), f32),
            pltpu.VMEM((n_x - 1, TWO_ROWS, width), f32),
            dma((8,)), dma((8,)), dma((10,)), dma((10,)), dma((2,)),
            dma((2, 2)), dma((2, 2)), dma((2, 2)), dma((2, 2)),
            dma((2, 2, n_x // 2, len(X_CUTS))), dma((2, 2, n_z // 2)), dma((2, 2, n_z // 2, LOTS_Z)), dma((2, n_x - 1)),
        ],
        compiler_params=pltpu.CompilerParams(
            collective_id=0, has_side_effects=True, vmem_limit_bytes=40 * 1024 * 1024),
    )(*small, item_factors.reshape(-1, BLK, width))


def solution(mesh):
    n_dp = mesh.shape["dp"]
    n_x = N_X
    n_z = n_dp // (2 * n_x)
    in_specs = (
        P(("dp", "rep"), None),
        P(("dp", "rep"), None),
        P(("dp", "rep"), None),
        P(("dp", "rep"), None),
        P("dp", "rep", None, None),
        P("dp", "rep", None),
        P(),
        P(),
    )
    return jax.shard_map(
        functools.partial(body, n_x, n_z), mesh=mesh, in_specs=in_specs,
        out_specs=P(("dp", "rep"), None), check_vma=False)
```

```python
import functools

import jax
import jax.numpy as jnp
from jax import lax
from jax.experimental import pallas as pl
from jax.experimental.pallas import tpu as pltpu
from jax.sharding import PartitionSpec as P

BLK = 64
CAP = 2
ITERS = 3
N_X = 4
PACKED_ROWS = 144
ONE_ROWS = 80
TWO_ROWS = PACKED_ROWS - ONE_ROWS
X_CUTS = (0, 1, 3, 5, 7, 11)
LOTS_Z = 4
MESH = pl.DeviceIdType.MESH
bf16, f32, i32 = jnp.bfloat16, jnp.float32, jnp.int32


def kernel(n_x, n_z, confidence_in, ratings_in, rated_in, owners_in, locals_in, hot_group_in, hot_local_in, items, out,
           confidence, ratings, rated, owners, locals_, hot_group, hot_local, pairs_of, lined, in_sem,
           table, staged, message, msg_z, passed, msg_x, ids, ids_z, ids_x, ids_s, one, two, one_x_half, one_x, one_z_half, one_z,
           two_z_half, two_z, two_x,
           y_send, y_recv, c_send, c_recv, l_sem, a_send, a_recv, b_send, b_recv,
           one_x_sem, one_z_sem, two_z_sem, two_x_sem):
    dp = lax.axis_index("dp")
    y = lax.axis_index("rep")
    core = dp % 2
    z = (dp // 2) % n_z
    x = dp // (2 * n_z)
    n_y = 4

    def at(x_to, z_to):
        return ((x_to * n_z + z_to) * 2 + core, y)

    up, down, far = (y + 1) % n_y, (y + n_y - 1) % n_y, (y + 2) % n_y
    up_id, down_id, mate_id = (dp, up), (dp, down), (x * n_z * 2 + z * 2 + 1 - core, y)

    def remote(src, dst, send, recv, to):
        return pltpu.make_async_remote_copy(
            src_ref=src, dst_ref=dst, send_sem=send, recv_sem=recv, device_id=to, device_id_type=MESH)

    def each(count, body):
        for k in range(1, count):
            body(k)

    def others(ref, lead=()):
        index = lead + (pl.ds(0, ref.shape[len(lead)] - 1),)
        return ref.at[index]

    def waiter(ref, send, recv):
        return remote(ref, ref, send, recv, mate_id)

    barrier = pltpu.get_barrier_semaphore()
    for k in sorted(range(1, n_z), key=lambda k: -min(k, n_z - k)):
        pl.semaphore_signal(barrier, inc=1, device_id=at(x, (z + k) % n_z), device_id_type=MESH)
    each(n_x, lambda k: pl.semaphore_signal(
        barrier, inc=1, device_id=at((x + k) % n_x, z), device_id_type=MESH))
    for to in (up_id, down_id, mate_id):
        pl.semaphore_signal(barrier, inc=1, device_id=to, device_id_type=MESH)

    given = (confidence_in, ratings_in, rated_in, owners_in, locals_in, hot_group_in, hot_local_in)
    held_in = (confidence, ratings, rated, owners, locals_, hot_group, hot_local)
    inputs = [pltpu.make_async_copy(a, b, in_sem.at[n]) for n, (a, b) in enumerate(zip(given, held_in))]
    for copy in inputs:
        copy.start()

    pairs = n_x * n_z
    for copy in inputs:
        copy.wait()
    cold, hot = owners.shape[1], hot_group.shape[1]
    listed = cold + hot
    width = listed + -listed % 128

    def row_of(cold_part, hot_part):
        return jnp.concatenate([cold_part, hot_part, jnp.zeros((1, width - listed), i32)], axis=1)

    owner_row = row_of(owners[...], hot_group[...] + 2 * pairs)
    local_row = row_of(locals_[...], hot_local[...])

    def two_blocks(k, carry):
        lanes = pl.ds(pl.multiple_of(128 * k, 128), 128)
        for n, given in enumerate((confidence, ratings)):
            lot = given[:, lanes].astype(f32)
            for u in range(2):
                pairs_of[2 * n + u, pl.ds(k, 1), :] = lot[u:u + 1]
        return carry

    lax.fori_loop(0, listed // 2, two_blocks, 0, unroll=4)
    for n in range(4):
        lined[n, pl.ds(listed, width - listed), :] = jnp.zeros((width - listed, 128), f32)
        lot = pairs_of[n]
        lined[n, pl.ds(0, listed // 2, stride=2), :] = lot
        lined[n, pl.ds(1, listed // 2, stride=2), :] = jnp.concatenate([lot[:, BLK:], lot[:, :BLK]], axis=1)
    owner_col = jnp.broadcast_to(owner_row, (8, width)).T[:, :1]
    before = lax.broadcasted_iota(i32, (width, width), 0) < lax.broadcasted_iota(i32, (width, width), 1)
    slot = jnp.sum(jnp.where((owner_col == owner_row) & before, 1, 0), axis=0, keepdims=True)
    number = lax.broadcasted_iota(i32, (1, width), 1)
    key = jnp.where(number < cold, owner_row * CAP + slot, jnp.where(number < listed, owner_row + 2 * pairs, -1))

    def wanted(pair, s):
        return 4 * pair + s if s < 4 else 4 * pairs + 2 * pair + s - 4

    entry = lax.broadcasted_iota(i32, (pairs, 1), 0)
    pair_of = (entry % n_x) * n_z + entry // n_x
    match = jnp.concatenate([key == wanted(pair_of, s) for s in range(6)], axis=0)
    rating_pick = jnp.where(match, 1.0, 0.0).astype(bf16)
    picked = []
    for u in range(2):
        rated_row = jnp.concatenate([rated[u:u + 1, :], jnp.zeros((1, width - listed), i32)], axis=1)
        weight_pick = jnp.where(match, rated_row.astype(f32), 0.0).astype(bf16)
        picked.append(jnp.dot(weight_pick, lined[u].astype(bf16), preferred_element_type=f32))
    for u in range(2):
        picked.append(jnp.dot(rating_pick, lined[2 + u].astype(bf16), preferred_element_type=f32))
    for n, lot in enumerate(picked):
        for j in range(3):
            both = [lot[(2 * j + i) * pairs:(2 * j + i + 1) * pairs, :BLK] for i in range(2)]
            staged[pl.ds(3 * n + j, pairs, stride=12), :] = jnp.concatenate(both, axis=1)
    message[...] = staged[...].astype(bf16).reshape(message.shape)
    to_z_entry = lax.broadcasted_iota(i32, (n_z, 1), 0)
    lane = lax.broadcasted_iota(i32, (n_z, 128), 1)
    id_rows = jnp.zeros((n_z, 128), i32)
    for x_to in range(n_x):
        for s in range(6):
            hit = jnp.where(key == wanted(x_to * n_z + to_z_entry, s), local_row, 0)
            id_rows = id_rows + jnp.where(lane == 8 * x_to + s, jnp.sum(hit, axis=1, keepdims=True), 0)
    for z_to in range(n_z):
        ids[z_to] = id_rows[z_to:z_to + 1]

    pl.semaphore_wait(barrier, 3 + n_z - 1 + n_x - 1)

    held = items.shape[0]
    half = held // 2

    def rows(of_core, of_y, h):
        return table.at[of_core, pl.ds(of_y * held + h * half, half)]

    fourth = half // 2

    def fourths(of_core, of_y, q):
        return table.at[of_core, pl.ds(of_y * held + q * fourth, fourth)]

    def own(h):
        return items.at[pl.ds(h * half, half)]

    def up_copy(k):
        if k < 2:
            return remote(own(k), rows(core, y, k), y_send.at[k], y_recv.at[k], up_id)
        return remote(fourths(core, down, k - 2), fourths(core, down, k - 2), y_send.at[k], y_recv.at[k], up_id)

    def down_copy(k):
        if k < 2:
            return remote(own(1 - k), rows(core, y, 1 - k), y_send.at[4 + k], y_recv.at[4 + k], down_id)
        return remote(fourths(core, up, k), fourths(core, up, k), y_send.at[4 + k], y_recv.at[4 + k], down_id)

    def from_down(k):
        ref = rows(core, down, k) if k < 2 else fourths(core, far, k - 2)
        return remote(ref, ref, y_send.at[k], y_recv.at[k], up_id)

    def from_up(k):
        ref = rows(core, up, 1 - k) if k < 2 else fourths(core, far, k)
        return remote(ref, ref, y_send.at[4 + k], y_recv.at[4 + k], down_id)

    def lot_of(n, of_core, of_y, h):
        return rows(of_core, of_y, h) if n < 6 else fourths(of_core, of_y, h)

    def mate_copy(n, src, of_y, h):
        return remote(src, lot_of(n, core, of_y, h), c_send.at[n], c_recv.at[n], mate_id)

    def from_mate(n, of_y, h):
        ref = lot_of(n, 1 - core, of_y, h)
        return remote(ref, ref, c_send.at[n], c_recv.at[n], mate_id)

    for k in range(2):
        up_copy(k).start()
        down_copy(k).start()
    keep = pltpu.make_async_copy(items, table.at[core, pl.ds(y * held, held)], l_sem.at[0])
    keep.start()

    def place_of(k):
        return 0 if 2 * k == n_z else (n_z - 2 * k if 2 * k < n_z else 2 * k - n_z - 1)

    outer = n_z // 2 - 1
    spans = (pl.ds(0, outer), pl.ds(outer, n_z - outer))
    counts = (outer, n_z - outer - 1)

    def start_z(k):
        to = (z + k) % n_z
        lot = 0 if place_of(k) < outer else 1
        remote(message.at[to], msg_z.at[place_of(k)], a_send.at[0, lot], a_recv.at[0, lot], at(x, to)).start()
        remote(ids.at[to], ids_z.at[place_of(k)], a_send.at[1, lot], a_recv.at[1, lot], at(x, to)).start()

    def start_x(k, lot):
        to = (x + k) % n_x
        remote(passed.at[to, spans[lot]], msg_x.at[x, spans[lot]], b_send.at[0, lot], b_recv.at[0, lot], at(to, z)).start()
        remote(ids_z.at[spans[lot]], ids_x.at[x, spans[lot]], b_send.at[1, lot], b_recv.at[1, lot], at(to, z)).start()

    z_done, x_done = [], []
    for lot in range(2):
        some = pl.ds(0, counts[lot])
        z_done.append([waiter(msg_z.at[some], a_send.at[0, lot], a_recv.at[0, lot]),
                       waiter(ids_z.at[some], a_send.at[1, lot], a_recv.at[1, lot])])
        some = pl.ds(0, n_x - 1)
        x_done.append([waiter(msg_x.at[some, spans[lot]], b_send.at[0, lot], b_recv.at[0, lot]),
                       waiter(ids_x.at[some, spans[lot]], b_send.at[1, lot], b_recv.at[1, lot])])

    def pass_on(lot):
        for copy in z_done[lot]:
            copy.wait_recv()

        def part(n, carry):
            text = msg_z[n].astype(f32)
            for x_to in range(n_x):
                rows_to = jnp.concatenate([text[12 * x_to:12 * x_to + 12], jnp.zeros((4, 128), f32)], axis=0)
                passed[x_to, n] = rows_to.astype(bf16)
            return carry

        lax.fori_loop(spans[lot].start, spans[lot].start + spans[lot].size, part, 0)
        each(n_x, lambda k: start_x(k, lot))
        msg_x[x, spans[lot]] = passed[x, spans[lot]]
        ids_x[x, spans[lot]] = ids_z[spans[lot]]

    for k in sorted(range(1, n_z), key=place_of):
        start_z(k)
    for h in range(2):
        mate_copy(h, own(h), y, h).start()
    msg_z[n_z - 1] = message[z]
    ids_z[n_z - 1] = ids[z]

    from_down(0).wait_recv()
    up_copy(2).start()
    up_copy(3).start()
    from_up(0).wait_recv()
    down_copy(2).start()
    down_copy(3).start()
    mate_copy(2, rows(core, down, 0), down, 0).start()
    mate_copy(3, rows(core, up, 1), up, 1).start()

    pass_on(0)
    pass_on(1)

    from_down(1).wait_recv()
    mate_copy(4, rows(core, down, 1), down, 1).start()
    from_up(1).wait_recv()
    mate_copy(5, rows(core, up, 0), up, 0).start()

    for copy in x_done[0] + x_done[1]:
        copy.wait_recv()
    to_smem = pltpu.make_async_copy(ids_x, ids_s, l_sem.at[1])
    to_smem.start()

    for k in range(2):
        from_down(2 + k).wait_recv()
        mate_copy(6 + 2 * k, fourths(core, far, k), far, k).start()
        from_up(2 + k).wait_recv()
        mate_copy(7 + 2 * k, fourths(core, far, 2 + k), far, 2 + k).start()

    for copy in z_done[0] + z_done[1] + x_done[0] + x_done[1]:
        copy.wait_send()
    for k in range(4):
        up_copy(k).wait_send()
        down_copy(k).wait_send()
    halves = [(y, 0), (y, 1), (down, 0), (up, 1), (down, 1), (up, 0), (far, 0), (far, 2), (far, 1), (far, 3)]
    for n, (of_y, h) in enumerate(halves):
        mate_copy(n, lot_of(n, core, of_y, h), of_y, h).wait_send()
    for n, (of_y, h) in enumerate(halves):
        from_mate(n, of_y, h).wait_recv()
    keep.wait()
    to_smem.wait()

    row_of = lax.broadcasted_iota(i32, (16, 128), 0)
    masks = [((row_of == 6 + j) | (row_of == 9 + j)).astype(f32) for j in range(3)]
    lane_block = lax.broadcasted_iota(i32, (8, 128), 1) // 8
    window = [(lane_block >= i) & (lane_block < i + 8) for i in range(8)]

    def build(place, carry):
        for p in range(n_x):
            build_one(p, place)
        return carry

    def build_one(p, place):
        xt = (x + (2, 1, 3, 0)[p]) % n_x
        found = [table[(0, 0, 1, 1, 0, 1)[s], ids_s[xt, place, 0, 8 * x + s]] for s in range(6)]
        chosen = jnp.concatenate(found, axis=0).T
        text = msg_x[xt, place].astype(f32)
        scaled = []
        for u in range(2):
            weight = jnp.concatenate(
                [jnp.broadcast_to(text[3 * u + j:3 * u + j + 1], (128, 128)) for j in range(3)], axis=1)
            scaled.append(chosen * weight.astype(bf16))
        scaled = jnp.concatenate(scaled, axis=0)
        rating = jnp.concatenate([(text * masks[j]).astype(bf16) for j in range(3)], axis=1)
        left = jnp.concatenate([chosen, rating], axis=0)
        both = lax.dot_general(left, scaled, (((1,), (1,)), ((), ())), preferred_element_type=f32)

        def group(u, i):
            return both[8 * i:8 * i + 8, 128 * u:128 * u + 128]

        main = [[jnp.where(window[i], group(u, i), group(u, i + 8)) for i in range(8)] for u in range(2)]
        shared = group(0, 0)
        for i in range(8):
            shared = jnp.where(lane_block == i + 8, group(0, i), shared)
            shared = jnp.where(lane_block == i, group(1, i + 8), shared)
        right = [
            jnp.sum(both[134 + 3 * u:137 + 3 * u, 128 * u:128 * u + 128], axis=0, keepdims=True)
            for u in range(2)
        ]
        packed = main[0] + main[1] + [shared, jnp.concatenate(right + [jnp.zeros((6, 128), f32)], axis=0)]
        one[p, place] = jnp.concatenate(packed[:one.shape[2] // 8], axis=0)
        two[p, place] = jnp.concatenate(packed[one.shape[2] // 8:], axis=0)

    last_x, last_z = n_x - 1, n_z - 1
    to_x = (at((x + 1) % n_x, z), at((x + n_x - 1) % n_x, z))
    to_z = (at(x, (z + 1) % n_z), at(x, (z + n_z - 1) % n_z))
    x_cuts = [cut for cut in X_CUTS if cut < n_z] + [n_z]
    x_lots = [pl.ds(cut, after - cut) for cut, after in zip(x_cuts, x_cuts[1:])]
    x_lot_of = [sum(cut <= n for cut in x_cuts) - 1 for n in range(n_z)]
    wide = n_x // LOTS_Z
    one_rows, two_rows = one.shape[2] // 2, two.shape[2] // 2
    steps_x, steps_z = n_x // 2, n_z // 2

    def place(way, step, steps):
        if step == steps:
            return 2 * steps - 1
        return 0 if step == 0 else 2 * step - 1 + way

    def one_x_copy(way, step, j):
        lots = x_lots[j]
        sems = one_x_sem.at[0, way, step, j], one_x_sem.at[1, way, step, j]
        if step == 0:
            return remote(one.at[0, lots, pl.ds(one_rows * way, one_rows)], one_x_half.at[way, lots], *sems, to_x[way])
        return remote(one.at[place(way, step, steps_x), lots], one_x.at[way, step - 1, lots], *sems, to_x[way])

    def one_z_copy(way, step):
        sems = one_z_sem.at[0, way, step], one_z_sem.at[1, way, step]
        if step == 0:
            return remote(one.at[last_x, 0, pl.ds(one_rows * way, one_rows)], one_z_half.at[way], *sems, to_z[way])
        return remote(one.at[last_x, place(way, step, steps_z)], one_z.at[way, step - 1], *sems, to_z[way])

    def two_z_copy(way, step, p):
        sems = two_z_sem.at[0, way, step, p], two_z_sem.at[1, way, step, p]
        lot = pl.ds(p * wide, wide)
        if step == 0:
            return remote(two.at[lot, 0, pl.ds(two_rows * way, two_rows)], two_z_half.at[way, lot], *sems, to_z[way])
        return remote(two.at[lot, place(way, step, steps_z)], two_z.at[way, step - 1, lot], *sems, to_z[way])

    def two_x_copy(p):
        ahead = (2, 1, 3)[p]
        sems = two_x_sem.at[0, p], two_x_sem.at[1, p]
        return remote(two.at[p, last_z], two_x.at[p], *sems, at((x + ahead) % n_x, z))

    delay, event_us, build_us = 2.5, 0.15, 0.5
    clock = {"now": 0.0, "x": 0.0, "z": 0.0}
    built, serial, pending, done_x, done_z = [0], [0], [], [], []

    def sent(axis, rows_sent, event, args):
        clock[axis] = max(clock[axis], clock["now"]) + rows_sent * 2 * 512 / 1e5
        serial[0] += 1
        pending.append((clock[axis] + delay, serial[0], event, args))

    def start_one_x(step, j):
        for way in range(2):
            one_x_copy(way, step, j).start()
        sent("x", x_lots[j].size * one_rows * (2 if step else 1), one_x_event, (step, j))

    def start_one_z(step):
        for way in range(2):
            one_z_copy(way, step).start()
        sent("z", one_rows * (2 if step else 1), one_z_event, (step,))

    def start_two_z(step, p):
        for way in range(2):
            two_z_copy(way, step, p).start()
        sent("z", wide * two_rows * (2 if step else 1), two_z_event, (step, p))

    def start_two_x():
        for p in range(last_x):
            two_x_copy(p).start()
        sent("x", 4 * two_rows, two_x_event, ())

    def ready_one_z():
        step = len(done_z)
        needed = x_lot_of[max(place(way, step, steps_z) for way in range(2))]
        if step < steps_z and set(range(needed + 1)) <= set(done_x) and ("one", step) not in begun:
            begun.add(("one", step))
            start_one_z(step)

    begun = set()

    def one_x_event(step, j):
        for way in range(2):
            one_x_copy(way, step, j).wait_recv()
            lots = x_lots[j]
            at_place = place(way, step + 1, steps_x)
            if step == 0:
                one[at_place, lots, pl.ds(one_rows * way, one_rows)] += one_x_half[way, lots]
            else:
                one[at_place, lots] += one_x[way, step - 1, lots]
            if step + 1 < steps_x:
                one_x_copy(way, step + 1, j).start()
        for way in range(2):
            one_x_copy(way, step, j).wait_send()
        if step + 1 < steps_x:
            sent("x", x_lots[j].size * one_rows * 2, one_x_event, (step + 1, j))
            if j + 2 < len(x_lots):
                first_one_x(j + 2)
        else:
            done_x.append(j)
            ready_one_z()

    def one_z_event(step):
        for way in range(2):
            one_z_copy(way, step).wait()
            at_place = place(way, step + 1, steps_z)
            if step == 0:
                one[last_x, at_place, pl.ds(one_rows * way, one_rows)] += one_z_half[way]
            else:
                one[last_x, at_place] += one_z[way, step - 1]
        done_z.append(step)
        ready_one_z()

    def two_z_event(step, p):
        lot = pl.ds(p * wide, wide)
        for way in range(2):
            two_z_copy(way, step, p).wait_recv()
            at_place = place(way, step + 1, steps_z)
            while at_place >= built[0]:
                build_some()
            if step == 0:
                two[lot, at_place, pl.ds(two_rows * way, two_rows)] += two_z_half[way, lot]
            else:
                two[lot, at_place] += two_z[way, step - 1, lot]
            if step + 1 < steps_z:
                two_z_copy(way, step + 1, p).start()
        for way in range(2):
            two_z_copy(way, step, p).wait_send()
        if step + 1 < steps_z:
            sent("z", wide * two_rows * 2, two_z_event, (step + 1, p))
        elif p == n_x // wide - 1:
            start_two_x()

    def two_x_event():
        for p in range(last_x):
            two_x_copy(p).wait()
        two[last_x, last_z] += two_x[0] + two_x[1] + two_x[2]

    def build_some():
        first = built[0]
        size = 1 if first == 0 else n_z // 4 - first % (n_z // 4)
        lax.fori_loop(first, first + size, build, 0)
        built[0] += size
        clock["now"] += build_us * size
        if first == 0:
            for p in range(n_x // wide):
                start_two_z(0, p)
        for j in range(min(2, len(x_lots))):
            if first < x_cuts[j + 1] <= built[0]:
                start_one_x(0, j)

    def first_one_x(j):
        while built[0] < x_cuts[j + 1]:
            build_some()
        start_one_x(0, j)

    while pending or built[0] < n_z:
        pending.sort()
        if built[0] < n_z and not (pending and pending[0][0] <= clock["now"]):
            build_some()
            continue
        arrival, _, event, args = pending.pop(0)
        clock["now"] = max(clock["now"], arrival) + event_us
        event(*args)

    row_block = lax.broadcasted_iota(i32, (128, 128), 0) // 8
    own_block = row_block == lax.broadcasted_iota(i32, (128, 128), 1) // 8
    lot = jnp.concatenate([one[last_x, last_z], two[last_x, last_z]], axis=0)
    grams = []
    for u in range(2):
        main = lot[64 * u:64 * u + 64]
        upper = [jnp.where(window[i], main[8 * i:8 * i + 8], 0.0) for i in range(8)]
        lower = [jnp.where(window[i], 0.0, main[8 * i:8 * i + 8]) for i in range(8)]
        for i in range(8):
            if u == 0:
                upper[i] = jnp.where(lane_block == i + 8, lot[128:136], upper[i])
            else:
                lower[i] = jnp.where(lane_block == i, lot[128:136], lower[i])
        kept = jnp.concatenate(upper + lower, axis=0)
        grams.append(kept + jnp.where(own_block, 0.0, kept).T)
    right = lot[136:138]

    def iterate(n, state):
        answer, residual, direction, norm = state
        turned = jnp.concatenate([direction, jnp.zeros((6, 128), f32)], axis=0).T
        image = jnp.concatenate(
            [jnp.sum(grams[u] * turned[:, u:u + 1], axis=0, keepdims=True) for u in range(2)], axis=0)
        image = image + 0.1 * direction
        step = norm / jnp.sum(direction * image, axis=-1, keepdims=True)
        answer = answer + step * direction
        residual = residual - step * image
        after = jnp.sum(residual * residual, axis=-1, keepdims=True)
        direction = residual + (after / norm) * direction
        return answer, residual, direction, after

    state = (jnp.zeros_like(right), right, right, jnp.sum(right * right, axis=-1, keepdims=True))
    for n in range(ITERS):
        state = iterate(n, state)
    out[...] = state[0]


def body(n_x, n_z, ratings, confidence, rated, item_factors, cold_owner, cold_local, hot_group, hot_local):
    users = confidence.shape[0]
    small = (confidence, ratings, rated, cold_owner.reshape(1, -1), cold_local.reshape(1, -1),
             hot_group.reshape(1, -1), hot_local.reshape(1, -1))
    listed = rated.shape[1]
    lines = listed + -listed % 128
    rows, width = item_factors.shape
    vmem = pl.BlockSpec(memory_space=pltpu.VMEM)
    dma = pltpu.SemaphoreType.DMA
    return pl.pallas_call(
        functools.partial(kernel, n_x, n_z),
        out_shape=jax.ShapeDtypeStruct((users, width), f32),
        in_specs=[pl.BlockSpec(memory_space=pl.ANY)] * 8,
        out_specs=vmem,
        scratch_shapes=[pltpu.VMEM(a.shape, a.dtype) for a in small] + [
            pltpu.VMEM((2 * users, listed // 2, width), f32),
            pltpu.VMEM((2 * users, lines, width), f32),
            dma((len(small),)),
            pltpu.VMEM((2, 4 * rows // BLK, BLK, width), bf16),
            pltpu.VMEM((n_z * n_x * 12, width), f32),
            pltpu.VMEM((n_z, n_x * 12, width), bf16),
            pltpu.VMEM((n_z, n_x * 12, width), bf16),
            pltpu.VMEM((n_x, n_z, 16, width), bf16),
            pltpu.VMEM((n_x, n_z, 16, width), bf16),
            pltpu.VMEM((n_z, 1, 128), i32),
            pltpu.VMEM((n_z, 1, 128), i32),
            pltpu.VMEM((n_x, n_z, 1, 128), i32),
            pltpu.SMEM((n_x, n_z, 1, 128), i32),
            pltpu.VMEM((n_x, n_z, ONE_ROWS, width), f32),
            pltpu.VMEM((n_x, n_z, TWO_ROWS, width), f32),
            pltpu.VMEM((2, n_z, ONE_ROWS // 2, width), f32),
            pltpu.VMEM((2, n_x // 2 - 1, n_z, ONE_ROWS, width), f32),
            pltpu.VMEM((2, ONE_ROWS // 2, width), f32),
            pltpu.VMEM((2, n_z // 2 - 1, ONE_ROWS, width), f32),
            pltpu.VMEM((2, n_x, TWO_ROWS // 2, width), f32),
            pltpu.VMEM((2, n_z // 2 - 1, n_x, TWO_ROWS, width), f32),
            pltpu.VMEM((n_x - 1, TWO_ROWS, width), f32),
            dma((8,)), dma((8,)), dma((10,)), dma((10,)), dma((2,)),
            dma((2, 2)), dma((2, 2)), dma((2, 2)), dma((2, 2)),
            dma((2, 2, n_x // 2, len(X_CUTS))), dma((2, 2, n_z // 2)), dma((2, 2, n_z // 2, LOTS_Z)), dma((2, n_x - 1)),
        ],
        compiler_params=pltpu.CompilerParams(
            collective_id=0, has_side_effects=True, vmem_limit_bytes=40 * 1024 * 1024),
    )(*small, item_factors.reshape(-1, BLK, width))


def solution(mesh):
    n_dp = mesh.shape["dp"]
    n_x = N_X
    n_z = n_dp // (2 * n_x)
    in_specs = (
        P(("dp", "rep"), None),
        P(("dp", "rep"), None),
        P(("dp", "rep"), None),
        P(("dp", "rep"), None),
        P("dp", "rep", None, None),
        P("dp", "rep", None),
        P(),
        P(),
    )
    return jax.shard_map(
        functools.partial(body, n_x, n_z), mesh=mesh, in_specs=in_specs,
        out_specs=P(("dp", "rep"), None), check_vma=False)
```
